32 devices in a mesh: shard: 4 (over x, core), rep: 8 (over z, y).
Axes of the slice: x: 2, y: 2, z: 4, core: 2. Of those that a mesh axis runs over, the one named last changes fastest.
Arguments:
- tokens: bfloat16 [32768, 576], P(('shard', 'rep')), may hold values from -6 to 6
- cotangent: bfloat16 [32768, 576], P(('shard', 'rep')), may hold values from -6 to 6
- segment_ids: int32 [32768], P(('shard', 'rep')), may hold values from 0 to 16, as said below
- current_attention: bfloat16 [576], replicated, may hold values from 0.5 to 1.5
- current_project: bfloat16 [576, 960], replicated, may hold values from -0.25 to 0.25
- current_output: bfloat16 [576, 576], replicated, may hold values from -2.5 to 2.5
- current_feeding: bfloat16 [576], replicated, may hold values from 0.5 to 1.5
- current_gating: bfloat16 [576, 1536], replicated, may hold values from -0.25 to 0.25
- current_upward: bfloat16 [576, 1536], replicated, may hold values from -0.25 to 0.25
- current_downward: bfloat16 [1536, 576], replicated, may hold values from -0.15625 to 0.15625
- master_attention: float32 [576], P('shard'), may hold values from 0.5 to 1.5
- master_project: float32 [576, 960], P('shard'), may hold values from -0.25 to 0.25
- master_output: float32 [576, 576], P('shard'), may hold values from -2.5 to 2.5
- master_feeding: float32 [576], P('shard'), may hold values from 0.5 to 1.5
- master_gating: float32 [576, 1536], P('shard'), may hold values from -0.25 to 0.25
- master_upward: float32 [576, 1536], P('shard'), may hold values from -0.25 to 0.25
- master_downward: float32 [1536, 576], P('shard'), may hold values from -0.15625 to 0.15625
- momentum_attention: float32 [576], P('shard'), may hold values from -0.046875 to 0.046875
- momentum_project: float32 [576, 960], P('shard'), may hold values from -0.046875 to 0.046875
- momentum_output: float32 [576, 576], P('shard'), may hold values from -0.00390625 to 0.00390625
- momentum_feeding: float32 [576], P('shard'), may hold values from -0.0078125 to 0.0078125
- momentum_gating: float32 [576, 1536], P('shard'), may hold values from -0.00390625 to 0.00390625
- momentum_upward: float32 [576, 1536], P('shard'), may hold values from -0.00390625 to 0.00390625
- momentum_downward: float32 [1536, 576], P('shard'), may hold values from -0.005859375 to 0.005859375
- variance_attention: float32 [576], P('shard'), may hold values from 7.324219e-05 to 0.0007324219
- variance_project: float32 [576, 960], P('shard'), may hold values from 7.324219e-05 to 0.0007324219
- variance_output: float32 [576, 576], P('shard'), may hold values from 4.882813e-07 to 4.8828124e-06
- variance_feeding: float32 [576], P('shard'), may hold values from 1.953125e-06 to 1.953125e-05
- variance_gating: float32 [576, 1536], P('shard'), may hold values from 4.882813e-07 to 4.8828124e-06
- variance_upward: float32 [576, 1536], P('shard'), may hold values from 4.882813e-07 to 4.8828124e-06
- variance_downward: float32 [1536, 576], P('shard'), may hold values from 1.0986328e-06 to 1.0986329e-05
Outputs:
- block_output: bfloat16 [32768, 576], P(('shard', 'rep'))
- tokens_gradient: bfloat16 [32768, 576], P(('shard', 'rep'))
- gradient_attention: float32 [576], P('shard')
- gradient_project: float32 [576, 960], P('shard')
- gradient_output: float32 [576, 576], P('shard')
- gradient_feeding: float32 [576], P('shard')
- gradient_gating: float32 [576, 1536], P('shard')
- gradient_upward: float32 [576, 1536], P('shard')
- gradient_downward: float32 [1536, 576], P('shard')
- updated_attention: float32 [576], P('shard')
- updated_project: float32 [576, 960], P('shard')
- updated_output: float32 [576, 576], P('shard')
- updated_feeding: float32 [576], P('shard')
- updated_gating: float32 [576, 1536], P('shard')
- updated_upward: float32 [576, 1536], P('shard')
- updated_downward: float32 [1536, 576], P('shard')
- velocity_attention: float32 [576], P('shard')
- velocity_project: float32 [576, 960], P('shard')
- velocity_output: float32 [576, 576], P('shard')
- velocity_feeding: float32 [576], P('shard')
- velocity_gating: float32 [576, 1536], P('shard')
- velocity_upward: float32 [576, 1536], P('shard')
- velocity_downward: float32 [1536, 576], P('shard')
- spread_attention: float32 [576], P('shard')
- spread_project: float32 [576, 960], P('shard')
- spread_output: float32 [576, 576], P('shard')
- spread_feeding: float32 [576], P('shard')
- spread_gating: float32 [576, 1536], P('shard')
- spread_upward: float32 [576, 1536], P('shard')
- spread_downward: float32 [1536, 576], P('shard')
- rounded_attention: bfloat16 [576], replicated
- rounded_project: bfloat16 [576, 960], replicated
- rounded_output: bfloat16 [576, 576], replicated
- rounded_feeding: bfloat16 [576], replicated
- rounded_gating: bfloat16 [576, 1536], replicated
- rounded_upward: bfloat16 [576, 1536], replicated
- rounded_downward: bfloat16 [1536, 576], replicated
The draws below stay inside these ranges and needn't reach their ends.
Inputs may be any that keep to these rules, and one draw needn't show every extreme that they name: `segment_ids`: within each sequence of 1024 rows the segment ids start at 0 and rise by one at each new document; every document has at least 60 tokens.
All inputs are finite; a program needn't handle non-finite values.
Results may differ from the reference program's by a relative error of at most 0.013.
Values may be sent and summed in bfloat16 or wider, within the bound.
A program may use at most 192 MiB of HBM per device.

```python
import math
import jax
import jax.numpy as jnp
from jax import lax

D = 576
H = 9
KV = 3
HS = 64
FF = 1536
TOK_DEV = 1024
DOC_MIN = 60
DOC_MAX = 800
STEP = 5
QKV = 960
TOKENS = 32768


def draw_segment_ids(key, part):
    key = jax.random.fold_in(key, 7)
    length_key = jax.random.fold_in(key, 1)
    pick_key = jax.random.fold_in(key, 2)
    sequences = TOKENS // TOK_DEV
    slot_count = TOK_DEV // DOC_MIN + 1
    lengths = jax.random.randint(length_key, (sequences, slot_count), DOC_MIN, DOC_MAX + 1)
    chosen = jax.random.randint(pick_key, (), 0, sequences)
    lengths = jnp.where(jnp.arange(sequences)[:, None] == chosen, DOC_MIN, lengths)
    doc_ends = jnp.cumsum(lengths, axis=1)
    doc_starts = jnp.where(doc_ends <= TOK_DEV - DOC_MIN, doc_ends, TOK_DEV + 1)
    places = jnp.arange(TOK_DEV, dtype=jnp.int32)
    segment_rows = jnp.sum((doc_starts[:, None, :] <= places[None, :, None]).astype(jnp.int32), axis=2)
    return segment_rows.reshape(TOKENS).astype(jnp.int32)


def block_levels(key, extent, split, low, top_value):
    factor_of = 1.0
    for position, shards_of in split:
        steps = jax.random.uniform(jax.random.fold_in(jax.random.fold_in(key, 6), position), (shards_of,), jnp.float32, low / len(split), top_value / len(split))
        factor_of = factor_of * jnp.repeat(jnp.exp(steps), extent[position] // shards_of).reshape((-1,) + (1,) * (len(extent) - 1 - position))
    return factor_of


def bell_draw(own_key, shape, scale, reach, cuts=(), held_as=jnp.bfloat16):
    result = scale * jax.random.normal(own_key, shape, jnp.float32)
    if cuts:
        result = result * block_levels(own_key, shape, cuts, -0.22, 0.18)
    return jnp.clip(result, -reach, reach).astype(held_as)


def setup_inputs(seed: int = 0) -> dict:
    seeds = jax.random.split(jax.random.key(seed), 32)
    return {
        "tokens": bell_draw(seeds[0], (TOKENS, D), 1.0, 6.0, ((0, 32),)),
        "cotangent": bell_draw(seeds[1], (TOKENS, D), 1.0, 6.0, ((0, 32),)),
        "segment_ids": draw_segment_ids(jax.random.fold_in(seeds[31], 71), 0),
        "current_attention": jnp.clip(1.0 + 0.1 * jax.random.normal(seeds[3], (D,), jnp.float32), 0.5, 1.5).astype(jnp.bfloat16),
        "current_project": bell_draw(seeds[4], (D, QKV), D ** -0.5, 0.25),
        "current_output": bell_draw(seeds[5], (D, D), (max(D // 96, 1)) ** -0.5, 2.5),
        "current_feeding": jnp.clip(1.0 + 0.1 * jax.random.normal(seeds[6], (D,), jnp.float32), 0.5, 1.5).astype(jnp.bfloat16),
        "current_gating": bell_draw(seeds[7], (D, FF), D ** -0.5, 0.25),
        "current_upward": bell_draw(seeds[8], (D, FF), D ** -0.5, 0.25),
        "current_downward": bell_draw(seeds[9], (FF, D), FF ** -0.5, 0.15625),
        "master_attention": jnp.clip(1.0 + 0.1 * jax.random.normal(seeds[10], (D,), jnp.float32), 0.5, 1.5),
        "master_project": bell_draw(seeds[11], (D, QKV), D ** -0.5, 0.25, ((0, 4),), jnp.float32),
        "master_output": bell_draw(seeds[12], (D, D), (max(D // 96, 1)) ** -0.5, 2.5, ((0, 4),), jnp.float32),
        "master_feeding": jnp.clip(1.0 + 0.1 * jax.random.normal(seeds[13], (D,), jnp.float32), 0.5, 1.5),
        "master_gating": bell_draw(seeds[14], (D, FF), D ** -0.5, 0.25, ((0, 4),), jnp.float32),
        "master_upward": bell_draw(seeds[15], (D, FF), D ** -0.5, 0.25, ((0, 4),), jnp.float32),
        "master_downward": bell_draw(seeds[16], (FF, D), FF ** -0.5, 0.15625, ((0, 4),), jnp.float32),
        "momentum_attention": bell_draw(seeds[17], (D,), (0.15 * (D // max(D // 96, 1)) ** 0.5 * TOKENS ** -0.5), 0.046875, ((0, 4),), jnp.float32),
        "momentum_project": bell_draw(seeds[18], (D, QKV), (0.15 * (D // max(D // 96, 1)) ** 0.5 * TOKENS ** -0.5), 0.046875, ((0, 4),), jnp.float32),
        "momentum_output": bell_draw(seeds[19], (D, D), (0.12 * TOKENS ** -0.5), 0.00390625, ((0, 4),), jnp.float32),
        "momentum_feeding": bell_draw(seeds[20], (D,), (0.24 * TOKENS ** -0.5), 0.0078125, ((0, 4),), jnp.float32),
        "momentum_gating": bell_draw(seeds[21], (D, FF), (0.12 * TOKENS ** -0.5), 0.00390625, ((0, 4),), jnp.float32),
        "momentum_upward": bell_draw(seeds[22], (D, FF), (0.12 * TOKENS ** -0.5), 0.00390625, ((0, 4),), jnp.float32),
        "momentum_downward": bell_draw(seeds[23], (FF, D), (0.18 * TOKENS ** -0.5), 0.005859375, ((0, 4),), jnp.float32),
        "variance_attention": jnp.clip(jnp.exp(math.log(0.0007324219) - 2.3025851 * jax.random.uniform(seeds[24], (D,), jnp.float32) ** block_levels(seeds[24], (D,), ((0, 4),), -0.2, 0.2)), 7.324219041038305e-05, 0.0007324219),
        "variance_project": jnp.clip(jnp.exp(math.log(0.0007324219) - 2.3025851 * jax.random.uniform(seeds[25], (D, QKV), jnp.float32) ** block_levels(seeds[25], (D, QKV), ((0, 4),), -0.2, 0.2)), 7.324219041038305e-05, 0.0007324219),
        "variance_output": jnp.clip(jnp.exp(math.log(4.882812390860636e-06) - 2.30258502 * jax.random.uniform(seeds[26], (D, D), jnp.float32) ** block_levels(seeds[26], (D, D), ((0, 4),), -0.2, 0.2)), 4.882812731921149e-07, 4.882812390860636e-06),
        "variance_feeding": jnp.clip(jnp.exp(math.log(1.9531249563442543e-05) - 2.30258502 * jax.random.uniform(seeds[27], (D,), jnp.float32) ** block_levels(seeds[27], (D,), ((0, 4),), -0.2, 0.2)), 1.9531250927684596e-06, 1.9531249563442543e-05),
        "variance_gating": jnp.clip(jnp.exp(math.log(4.882812390860636e-06) - 2.30258502 * jax.random.uniform(seeds[28], (D, FF), jnp.float32) ** block_levels(seeds[28], (D, FF), ((0, 4),), -0.2, 0.2)), 4.882812731921149e-07, 4.882812390860636e-06),
        "variance_upward": jnp.clip(jnp.exp(math.log(4.882812390860636e-06) - 2.30258502 * jax.random.uniform(seeds[29], (D, FF), jnp.float32) ** block_levels(seeds[29], (D, FF), ((0, 4),), -0.2, 0.2)), 4.882812731921149e-07, 4.882812390860636e-06),
        "variance_downward": jnp.clip(jnp.exp(math.log(1.0986328561557457e-05) - 2.3025852 * jax.random.uniform(seeds[30], (FF, D), jnp.float32) ** block_levels(seeds[30], (FF, D), ((0, 4),), -0.2, 0.2)), 1.0986327652062755e-06, 1.0986328561557457e-05),
    }


EPSILON = 1e-05
THETA = 10000.0
BETA = 0.5
ADAM_EPSILON = 1e-08
DECAY = 0.1
NEGATIVE = -1e+30
BASE_RATE = 0.3

@jax.custom_vjp
def low(v):
    return lax.optimization_barrier(v.astype(jnp.bfloat16)).astype(jnp.float32)

@jax.custom_vjp
def low_back(v):
    return v

def low_keep(v):
    return (low(v), None)

def low_pass(kept, grad):
    return (grad,)

def back_keep(v):
    return (v, None)

def back_low(kept, grad):
    return (low(grad),)
low.defvjp(low_keep, low_pass)
low_back.defvjp(back_keep, back_low)

def product(left, right):
    return jnp.dot(left, right, precision=lax.Precision.HIGHEST)

def normalize(values, gain):
    return values * lax.rsqrt(lax.optimization_barrier(jnp.mean(values * values, axis=-1, keepdims=True)) + EPSILON) * gain

def positions_of(segment):
    places = jnp.arange(segment.shape[0], dtype=jnp.int32)
    before = jnp.concatenate([segment[:1] - 1, segment[:-1]])
    starts = jnp.where(segment != before, places, 0)
    return places - lax.cummax(starts, axis=0)

def rope_tables(segment):
    half_size = HS // 2
    places = positions_of(segment).astype(jnp.float32)
    frequency = jnp.exp(jnp.arange(half_size, dtype=jnp.float32) * (-2.0 * math.log(THETA) / HS))
    angles = places[:, None] * frequency[None, :]
    return (jnp.cos(angles), jnp.sin(angles))

def rotate(values, cosine_table, sine_table):
    half_size = values.shape[-1] // 2
    first_half = values[..., :half_size]
    second_half = values[..., half_size:]
    return jnp.concatenate([first_half * cosine_table - second_half * sine_table, second_half * cosine_table + first_half * sine_table], axis=-1)

def rate_scales():
    return (1.0, float(D) ** (-0.5), float(max(D // 96, 1)) ** (-0.5), 1.0, float(D) ** (-0.5), float(D) ** (-0.5), float(FF) ** (-0.5))

def forward(inputs_float, attention, project, output, feeding, gating, upward, downward, segment, cosine_table, sine_table):
    rows_count = inputs_float.shape[0]
    group_size = H // KV
    score_scale = 1.0 / math.sqrt(HS)
    normed = low(normalize(inputs_float, attention))
    joined = low_back(product(normed, project))
    queries = joined[:, :H * HS].reshape(rows_count, KV, group_size, HS)
    key_rows = joined[:, H * HS:(H + KV) * HS].reshape(rows_count, KV, HS)
    value_rows = low(joined[:, (H + KV) * HS:].reshape(rows_count, KV, HS))
    queries = low(rotate(queries, cosine_table[:, None, None, :], sine_table[:, None, None, :]))
    key_rows = low(rotate(key_rows, cosine_table[:, None, :], sine_table[:, None, :]))
    scores = low_back(jnp.einsum('qngd,knd->ngqk', queries, key_rows, precision=lax.Precision.HIGHEST) * score_scale)
    places = jnp.arange(rows_count)
    allowed = (segment[:, None] == segment[None, :]) & (places[:, None] >= places[None, :])
    probability = jax.nn.softmax(jnp.where(allowed, scores, NEGATIVE), axis=-1)
    mixed_rows = jnp.einsum('ngqk,knd->qngd', low(probability), value_rows, precision=lax.Precision.HIGHEST)
    mixed_rows = low_back(low(mixed_rows.reshape(rows_count, H * HS)))
    residual = inputs_float + low_back(product(mixed_rows, output))
    normed_two = low(normalize(residual, feeding))
    gate_values = low_back(product(normed_two, gating))
    up_values = low_back(product(normed_two, upward))
    hidden = low(jax.nn.silu(gate_values) * up_values)
    return residual + low_back(product(hidden, downward))

def reference(tokens, cotangent, segment_ids, current_attention, current_project, current_output, current_feeding, current_gating, current_upward, current_downward, master_attention, master_project, master_output, master_feeding, master_gating, master_upward, master_downward, momentum_attention, momentum_project, momentum_output, momentum_feeding, momentum_gating, momentum_upward, momentum_downward, variance_attention, variance_project, variance_output, variance_feeding, variance_gating, variance_upward, variance_downward):
    currents = tuple((w.astype(jnp.float32) for w in (current_attention, current_project, current_output, current_feeding, current_gating, current_upward, current_downward)))
    inputs_all = tokens.astype(jnp.float32).reshape(-1, TOK_DEV, D)
    cotangent_all = cotangent.astype(jnp.float32).reshape(-1, TOK_DEV, D)
    segment_all = segment_ids.reshape(-1, TOK_DEV)

    def one_sequence(totals, pieces):
        inputs_float, cotangent_float, segment = pieces
        cosine_table, sine_table = rope_tables(segment)

        def apply_block(inputs_value, *params):
            return forward(inputs_value, *params, segment, cosine_table, sine_table)
        outputs, pullback = jax.vjp(apply_block, inputs_float, *currents)
        grads = pullback(cotangent_float)
        totals = tuple((left + right for left, right in zip(totals, grads[1:])))
        return (totals, (outputs.astype(jnp.bfloat16), grads[0].astype(jnp.bfloat16)))
    zero_sums = tuple((jnp.zeros_like(w) for w in currents))
    totals, (output_rows, grad_rows) = lax.scan(one_sequence, zero_sums, (inputs_all, cotangent_all, segment_all))
    gradients = tuple((whole_sum / TOKENS for whole_sum in totals))
    masters = (master_attention, master_project, master_output, master_feeding, master_gating, master_upward, master_downward)
    moments = (momentum_attention, momentum_project, momentum_output, momentum_feeding, momentum_gating, momentum_upward, momentum_downward)
    variances = (variance_attention, variance_project, variance_output, variance_feeding, variance_gating, variance_upward, variance_downward)
    scales = rate_scales()
    correction = 1.0 - BETA ** STEP
    velocities = []
    spreads = []
    updates = []
    for number in range(7):
        grad_value = gradients[number]
        rate = BASE_RATE * scales[number]
        velocity = BETA * moments[number] + (1.0 - BETA) * grad_value
        spread = BETA * variances[number] + (1.0 - BETA) * grad_value * grad_value
        direction = velocity / correction / (jnp.sqrt(spread / correction) + ADAM_EPSILON)
        if number in (0, 3):
            updated = masters[number] - rate * direction
        else:
            updated = masters[number] - rate * (direction + DECAY * masters[number])
        velocities.append(velocity)
        spreads.append(spread)
        updates.append(updated)
    rounded = [u.astype(jnp.bfloat16) for u in updates]
    return (output_rows.reshape(TOKENS, D), grad_rows.reshape(TOKENS, D), gradients[0], gradients[1], gradients[2], gradients[3], gradients[4], gradients[5], gradients[6], updates[0], updates[1], updates[2], updates[3], updates[4], updates[5], updates[6], velocities[0], velocities[1], velocities[2], velocities[3], velocities[4], velocities[5], velocities[6], spreads[0], spreads[1], spreads[2], spreads[3], spreads[4], spreads[5], spreads[6], rounded[0], rounded[1], rounded[2], rounded[3], rounded[4], rounded[5], rounded[6])
```

```python
import math

import jax
import jax.numpy as jnp
from jax import lax
from jax.experimental import pallas as pl
from jax.experimental.pallas import tpu as pltpu
from jax.sharding import PartitionSpec as P

D = 576
H = 9
KV = 3
HS = 64
FF = 1536
QKV = 960
STEP = 5
GROUP = H // KV

EPSILON = 1e-05
THETA = 10000.0
BETA = 0.5
ADAM_EPSILON = 1e-08
DECAY = 0.1
NEGATIVE = -1e30
BASE_RATE = 0.3

F32 = jnp.float32
BF16 = jnp.bfloat16
T = 256
PR = D // 4
PC = FF // 4


def dot(a, b):
    return jnp.dot(a, b, preferred_element_type=F32)


def dot_t(a, b):
    return lax.dot_general(a, b, (((1,), (1,)), ((), ())), preferred_element_type=F32)


def column(ref, size):
    row = jnp.broadcast_to(ref[...].astype(F32).reshape(1, size), (8, size))
    return row.T[:, :1]


def block_kernel(
    xt_ref, ct_ref, seg_ref, g1_ref, g2_ref, wp_ref, wo_ref, wg_ref, wu_ref, wdt_ref,
    bot_ref, tgt_ref, gain_ref, gr_ref,
    qt, kt_, vt, kn, vn, nt, mt, gmt, et, eb, invl, gres, dgain,
):
    rows = xt_ref.shape[1]
    tiles = rows // T
    half = HS // 2

    seg_row = seg_ref[...].astype(F32)
    seg_cols = jnp.broadcast_to(seg_row, (8, rows)).T[:, :1]
    starts = jnp.zeros((1, rows), F32)
    for k in range(0, rows, 128):
        lower = (seg_cols[k : k + 128] < seg_row).astype(F32)
        starts = starts + jnp.sum(lower, axis=0, keepdims=True)
    places_row = lax.broadcasted_iota(jnp.int32, (1, rows), 1).astype(F32)
    index = lax.broadcasted_iota(jnp.int32, (half, 1), 0).astype(F32)
    frequency = jnp.exp(index * (-2.0 * math.log(THETA) / HS))
    angles = frequency * (places_row - starts)
    cosine = jnp.cos(angles)
    sine = jnp.sin(angles)

    gain1 = column(g1_ref, D)
    gain2 = column(g2_ref, D)
    dgain[...] = jnp.zeros_like(dgain)

    def unit_one(cols):
        xf = xt_ref[:, cols].astype(F32)
        scale = lax.rsqrt(jnp.mean(xf * xf, axis=0, keepdims=True) + EPSILON)
        return xf * scale, scale

    def project(wpt):
        wpt[...] = wp_ref[...].T
        for r in range(tiles):
            r0 = r * T
            cs = cosine[:, r0 : r0 + T]
            sn = sine[:, r0 : r0 + T]
            unit, _ = unit_one(slice(r0, r0 + T))
            normed = (unit * gain1).astype(BF16)
            nt[:, r0 : r0 + T] = normed
            joined = dot(wpt[...], normed)
            for h in range(H + 2 * KV):
                jt = joined[h * HS : (h + 1) * HS]
                a = jt[:half]
                b = jt[half:]
                if h < H:
                    qt[h, 0:half, r0 : r0 + T] = ((a * cs - b * sn) * (HS**-0.5)).astype(BF16)
                    qt[h, half:HS, r0 : r0 + T] = ((b * cs + a * sn) * (HS**-0.5)).astype(BF16)
                elif h < H + KV:
                    kt_[h - H, 0:half, r0 : r0 + T] = (a * cs - b * sn).astype(BF16)
                    kt_[h - H, half:HS, r0 : r0 + T] = (b * cs + a * sn).astype(BF16)
                else:
                    vt[h - H - KV, :, r0 : r0 + T] = jt.astype(BF16)

    pl.run_scoped(project, pltpu.VMEM((QKV, D), BF16))
    for n in range(KV):
        kn[n] = kt_[n].T
        vn[n] = vt[n].T

    def ef(k, i):
        if k < 2:
            return et, k * T, i * T
        return eb, (k - 2) * T, (i - 2) * T

    def forward(bias, sc):
        for i in range(tiles):
            for k in range(i + 1):
                kk = lax.broadcasted_iota(jnp.int32, (T, T), 0).astype(F32) + float(k * T)
                ok = kk >= starts[:, i * T : (i + 1) * T]
                if k == i:
                    qq = lax.broadcasted_iota(jnp.int32, (T, T), 1).astype(F32) + float(i * T)
                    ok = ok & (kk <= qq)
                bias[i * (i + 1) // 2 + k] = jnp.where(ok, 0.0, NEGATIVE)

        def head(h, _):
            n = h // GROUP
            for i in range(tiles):
                q = qt[h, :, i * T : (i + 1) * T]
                peak = None
                for k in range(i + 1):
                    s = dot(kn[n, k * T : (k + 1) * T, :], q) + bias[i * (i + 1) // 2 + k]
                    sc[i % 2, k] = s
                    top = jnp.max(s, axis=0, keepdims=True)
                    peak = top if peak is None else jnp.maximum(peak, top)
                total = jnp.zeros((1, T), F32)
                out = jnp.zeros((HS, T), F32)
                for k in range(i + 1):
                    e = jnp.exp(sc[i % 2, k] - peak)
                    total = total + jnp.sum(e, axis=0, keepdims=True)
                    e16 = e.astype(BF16)
                    ref, a, b = ef(k, i)
                    ref[h, a : a + T, b : b + T] = e16
                    out = out + dot(vt[n, :, k * T : (k + 1) * T], e16)
                inverse = 1.0 / total
                invl[h, :, i * T : (i + 1) * T] = inverse
                mt[pl.ds(pl.multiple_of(h * HS, HS), HS), i * T : (i + 1) * T] = (
                    out * inverse
                ).astype(BF16)
            return 0

        lax.fori_loop(0, H, head, 0)

    pl.run_scoped(
        forward,
        pltpu.VMEM((tiles * (tiles + 1) // 2, T, T), F32),
        pltpu.VMEM((2, tiles, T, T), F32),
    )

    RT = 512
    CT = 256

    def feeding(wot, cn, n2, n2t, hid, gg, gu, res):
        wot[...] = wo_ref[...].T
        cn[...] = ct_ref[...].T

        def rowtile(r, _):
            rs = pl.ds(pl.multiple_of(r * RT, RT), RT)
            residual = xt_ref[:, rs].astype(F32) + dot(wot[...], mt[:, rs])
            scale = lax.rsqrt(jnp.mean(residual * residual, axis=0, keepdims=True) + EPSILON)
            res[...] = residual
            n2v = (residual * scale * gain2).astype(BF16)
            n2t[:, rs] = n2v
            n2[...] = n2v.T

            def col(j, _):
                js = pl.ds(pl.multiple_of(j * CT, CT), CT)
                gate = dot(n2[...], wg_ref[:, js])
                up = dot(n2[...], wu_ref[:, js])
                gh = dot(cn[rs, :], wdt_ref[:, js])
                sg = 0.5 * jnp.tanh(0.5 * gate) + 0.5
                sl = gate * sg
                hid[rs, js] = (sl * up).astype(BF16)
                gg[rs, js] = (gh * up * (sg + sl * (1.0 - sg))).astype(BF16)
                gu[rs, js] = (gh * sl).astype(BF16)
                return 0

            lax.fori_loop(0, FF // CT, col, 0)
            residual = res[...]
            bot_ref[:, rs] = (residual + dot_t(wdt_ref[...], hid[rs, :])).astype(BF16)
            gn2 = dot_t(wg_ref[...], gg[rs, :]) + dot_t(wu_ref[...], gu[rs, :])
            unit = residual * scale
            dgain[:, 1:2] += jnp.sum(gn2 * unit, axis=1, keepdims=True)
            e = gn2 * gain2
            gr = ct_ref[:, rs].astype(F32) + scale * (
                e - unit * jnp.mean(e * unit, axis=0, keepdims=True)
            )
            gres[:, rs] = gr
            gmt[:, rs] = dot(wo_ref[...], gr.astype(BF16)).astype(BF16)
            return 0

        lax.fori_loop(0, rows // RT, rowtile, 0)

        def wide(j, _):
            js = pl.ds(pl.multiple_of(j * PC, PC), PC)
            gr_ref[2, j] = dot(ct_ref[...], hid[:, js]).astype(BF16).reshape(4, PR, PC)
            gr_ref[0, :, j] = dot(n2t[...], gg[:, js]).astype(BF16).reshape(4, PR, PC)
            gr_ref[1, :, j] = dot(n2t[...], gu[:, js]).astype(BF16).reshape(4, PR, PC)
            return 0

        lax.fori_loop(0, FF // PC, wide, 0)
        gr_ref[3, :, 3] = dot_t(mt[...], gres[:PC].astype(BF16)).astype(BF16).reshape(4, PR, PC)
        part = dot_t(mt[...], gres[PC:].astype(BF16)).astype(BF16)
        gr_ref[3, :, 2, :, PC // 2 :] = part.reshape(4, PR, PC // 2)

    pl.run_scoped(
        feeding,
        pltpu.VMEM((D, D), BF16),
        pltpu.VMEM((rows, D), BF16),
        pltpu.VMEM((RT, D), BF16),
        pltpu.VMEM((D, rows), BF16),
        pltpu.VMEM((rows, FF), BF16),
        pltpu.VMEM((rows, FF), BF16),
        pltpu.VMEM((rows, FF), BF16),
        pltpu.VMEM((D, RT), F32),
    )

    def backward(ds, gjt, dk, dv, cs_ref, sn_ref):
        cs_ref[...] = cosine
        sn_ref[...] = sine

        def unrotate(v, base):
            a = v[:half]
            b = v[half:]
            cs = cs_ref[...]
            sn = sn_ref[...]
            gjt[pl.ds(pl.multiple_of(base, HS), half), :] = (a * cs + b * sn).astype(BF16)
            gjt[pl.ds(pl.multiple_of(base + half, half), half), :] = (b * cs - a * sn).astype(BF16)

        def head(h, _):
            n = h // GROUP
            hs = pl.ds(pl.multiple_of(h * HS, HS), HS)
            first = lax.rem(h, GROUP) == 0

            @pl.when(first)
            def _():
                dk[...] = jnp.zeros_like(dk)
                dv[...] = jnp.zeros_like(dv)

            do = (gmt[hs, :].astype(F32) * invl[h]).astype(BF16)
            delta = jnp.sum(do.astype(F32) * mt[hs, :].astype(F32), axis=0, keepdims=True)
            for k in range(tiles):
                ks = slice(k * T, (k + 1) * T)
                for i in range(k, tiles):
                    cols = slice(i * T, (i + 1) * T)
                    ref, a, b = ef(k, i)
                    dp = dot(vn[n, ks, :], do[:, cols]) - delta[:, cols]
                    ds[ks, cols] = (ref[h, a : a + T, b : b + T].astype(F32) * dp).astype(BF16)
                ref, a, b = ef(k, k)
                dv[ks, :] += dot_t(ref[h, a : a + T, b : b + rows - k * T], do[:, k * T :])
                dk[ks, :] += dot_t(ds[ks, k * T :], qt[h, :, k * T :])
            dq = [
                dot(kt_[n, :, : (i + 1) * T], ds[: (i + 1) * T, i * T : (i + 1) * T])
                for i in range(tiles)
            ]
            unrotate(jnp.concatenate(dq, axis=1) * (HS**-0.5), h * HS)

            @pl.when(lax.rem(h, GROUP) == GROUP - 1)
            def _():
                unrotate(dk[...].T, H * HS + n * HS)
                gjt[pl.ds(pl.multiple_of((H + KV + n) * HS, HS), HS), :] = dv[...].T.astype(BF16)

            return 0

        lax.fori_loop(0, H, head, 0)

        for p in range(2):
            part = dot_t(nt[...], gjt[p * PC : (p + 1) * PC, :]).astype(BF16)
            gr_ref[3, :, p] = part.reshape(4, PR, PC)
        part = dot_t(nt[...], gjt[2 * PC :, :]).astype(BF16)
        gr_ref[3, :, 2, :, : PC // 2] = part.reshape(4, PR, PC // 2)

        def rowtile(r, _):
            rs = pl.ds(pl.multiple_of(r * T, T), T)
            gn = dot(wp_ref[...], gjt[:, rs])
            unit, scale = unit_one(rs)
            dgain[:, 0:1] += jnp.sum(gn * unit, axis=1, keepdims=True)
            e = gn * gain1
            tg = gres[:, rs] + scale * (e - unit * jnp.mean(e * unit, axis=0, keepdims=True))
            tgt_ref[:, rs] = tg.astype(BF16)
            return 0

        lax.fori_loop(0, rows // T, rowtile, 0)
        for s in range(4):
            gain_ref[s] = dgain[s * PR : (s + 1) * PR, :].T

    pl.run_scoped(
        backward,
        pltpu.VMEM((rows, rows), BF16),
        pltpu.VMEM((QKV, rows), BF16),
        pltpu.VMEM((rows, HS), F32),
        pltpu.VMEM((rows, HS), F32),
        pltpu.VMEM((half, rows), F32),
        pltpu.VMEM((half, rows), F32),
    )


def run_block(xt, ct, seg, g1, g2, wp, wo, wg, wu, wdt):
    rows = xt.shape[1]
    vm = pl.BlockSpec(memory_space=pltpu.VMEM)
    sd = jax.ShapeDtypeStruct
    return pl.pallas_call(
        block_kernel,
        name="block",
        out_shape=(
            sd((D, rows), BF16),
            sd((D, rows), BF16),
            sd((4, 8, PR), F32),
            sd((4, 4, 4, PR, PC), BF16),
        ),
        in_specs=[vm] * 10,
        out_specs=(vm,) * 4,
        scratch_shapes=[
            pltpu.VMEM((H, HS, rows), BF16),
            pltpu.VMEM((KV, HS, rows), BF16),
            pltpu.VMEM((KV, HS, rows), BF16),
            pltpu.VMEM((KV, rows, HS), BF16),
            pltpu.VMEM((KV, rows, HS), BF16),
            pltpu.VMEM((D, rows), BF16),
            pltpu.VMEM((D, rows), BF16),
            pltpu.VMEM((D, rows), BF16),
            pltpu.VMEM((H, 2 * T, rows), BF16),
            pltpu.VMEM((H, 2 * T, rows - 2 * T), BF16),
            pltpu.VMEM((H, 1, rows), F32),
            pltpu.VMEM((D, rows), F32),
            pltpu.VMEM((D, 8), F32),
        ],
        compiler_params=pltpu.CompilerParams(vmem_limit_bytes=62 * 2**20),
    )(xt, ct, seg.reshape(1, rows), g1, g2, wp, wo, wg, wu, wdt)
MESH = pl.DeviceIdType.MESH
SPLIT = 80
RATES = tuple(
    BASE_RATE * v
    for v in (float(D) ** -0.5, float(D) ** -0.5, float(FF) ** -0.5, float(D) ** -0.5, float(max(D // 96, 1)) ** -0.5)
)
CORRECTION = 1.0 - BETA**STEP


def adam(grad, master, moment, variance, rate, decay):
    velocity = BETA * moment + (1.0 - BETA) * grad
    spread = BETA * variance + (1.0 - BETA) * grad * grad
    direction = velocity / CORRECTION / (jnp.sqrt(spread / CORRECTION) + ADAM_EPSILON)
    if decay:
        direction = direction + DECAY * master
    return velocity, spread, master - rate * direction


def places(t, p):
    if t < 2:
        return [(0, t, 0, p * PC, PR, PC)]
    if t == 2:
        return [(0, 2, p * PR, 0, PR, PC)]
    if p < 2:
        return [(0, 3, 0, p * PC, PR, PC)]
    if p == 2:
        return [(0, 3, 0, 2 * PC, PR, PC // 2), (PC // 2, 4, 0, PC, PR, PC // 2)]
    return [(0, 4, 0, 0, PR, PC)]


def add_into(dst, a, b):
    dst[...] = (a[...].astype(F32) + b[...].astype(F32)).astype(BF16)


def exchange_kernel(bits, total, *refs):
    gr_ref, gain_ref = refs[:2]
    state = refs[2:17]
    gain_state = refs[17:23]
    gf_ref, u_ref, gsum_ref, gup_ref = refs[23:27]
    (s1, r1, s2a, r2a, s2b, r2b, s3, r3, s4, r4, r5, s5, up, gs, grc, gu) = refs[27:43]
    held = refs[43:58]
    send_sem, recv_sem, load_sem, keep_sem = refs[58:62]

    shard = lax.axis_index("shard")
    rep = lax.axis_index("rep")
    x, core = shard // 2, lax.rem(shard, 2)
    y, zl = lax.rem(rep, 2), lax.rem(rep // 2, 2)

    def flip(index, bit):
        size = 1 << bit
        return index + size - 2 * size * lax.rem(index // size, 2)

    peer_c = (flip(shard, 0), rep)
    peer_x = (flip(shard, 1), rep)
    peer_r = [(shard, flip(rep, b)) for b in range(bits)]
    peers = [peer_c, peer_x] + peer_r

    loads = []
    for number in range(15):
        loads.append(pltpu.make_async_copy(state[number], held[number], load_sem.at[number]))
        loads[-1].start()

    barrier = pltpu.get_barrier_semaphore()
    for peer in peers:
        pl.semaphore_signal(barrier, inc=1, device_id=peer, device_id_type=MESH)
    pl.semaphore_wait(barrier, len(peers))

    sent = []

    def send(src, dst, peer):
        n = len(sent)
        copy = pltpu.make_async_remote_copy(
            src_ref=src, dst_ref=dst, send_sem=send_sem.at[n], recv_sem=recv_sem.at[n],
            device_id=peer, device_id_type=MESH,
        )
        copy.start()
        sent.append(copy)
        return copy

    keeps = []

    def gain_flow():
        copy = send(gain_ref, grc.at[0], peer_c)
        yield
        for b, peer in enumerate(peers):
            copy.wait_recv()
            gs[b] = (gain_ref[...] if b == 0 else gs[b - 1]) + grc[b]
            if b + 1 < len(peers):
                copy = send(gs.at[b], grc.at[b + 1], peers[b + 1])
                yield
        gsum_ref[...] = gs[len(peers) - 1]
        grad = gs[len(peers) - 1, shard] / total
        for k in range(2):
            m, v, w = (gain_state[2 * q + k][...].reshape(1, PR) for q in range(3))
            gu[shard, k : k + 1, :] = adam(grad[k : k + 1], m, v, w, BASE_RATE, False)[2]
        copy = send(gu.at[shard], gu.at[shard], peer_x)
        yield
        copy.wait_recv()
        one = send(gu.at[shard], gu.at[shard], peer_c)
        two = send(gu.at[flip(shard, 1)], gu.at[flip(shard, 1)], peer_c)
        yield
        one.wait_recv()
        two.wait_recv()
        gup_ref[...] = gu[...]

    def flow(t):
        copies = [
            send(gr_ref.at[t, 2 * i + 1 - core], r1.at[t, i], peer_c) for i in range(2)
        ]
        yield
        for copy in copies:
            copy.wait_recv()
        for i in range(2):
            def step(p, _):
                add_into(s1.at[t, i, p], gr_ref.at[t, 2 * i + core, p], r1.at[t, i, p])
                return 0

            lax.fori_loop(0, 4, step, 0)
        a, b = pl.ds(0, SPLIT), pl.ds(SPLIT, PR - SPLIT)
        one = send(s1.at[t, 1 - x, :, a], r2a.at[t], peer_x)
        two = send(s1.at[t, :, pl.ds(2 * (1 - y), 2), b], r2b.at[t], peer_r[0])
        yield
        one.wait_recv()
        two.wait_recv()
        for p in range(4):
            add_into(s2a.at[t, p], s1.at[t, x, p, a], r2a.at[t, p])
        for i in range(2):
            for q in range(2):
                add_into(s2b.at[t, i, q], s1.at[t, i, 2 * y + q, b], r2b.at[t, i, q])
        one = send(s2a.at[t, pl.ds(2 * (1 - y), 2)], r3.at[t, :, a], peer_r[0])
        two = send(s2b.at[t, 1 - x], r3.at[t, :, b], peer_x)
        yield
        one.wait_recv()
        two.wait_recv()
        for q in range(2):
            add_into(s3.at[t, q, a], s2a.at[t, 2 * y + q], r3.at[t, q, a])
            add_into(s3.at[t, q, b], s2b.at[t, x, q], r3.at[t, q, b])
        copy = send(s3.at[t, 1 - zl], r4.at[t], peer_r[1])
        yield
        copy.wait_recv()
        add_into(s4.at[t, 0], s3.at[t, zl], r4.at[t])
        for k in range(bits - 2):
            copy = send(s4.at[t, k], r5.at[t, k], peer_r[2 + k])
            yield
            copy.wait_recv()
            add_into(s4.at[t, k + 1], s4.at[t, k], r5.at[t, k])
        mine = 2 * y + zl
        s5[t, mine] = s4[t, bits - 2]
        copy = send(s4.at[t, bits - 2], s5.at[t, mine], peer_r[1])
        yield
        copy.wait_recv()
        copy = send(s5.at[t, pl.ds(2 * y, 2)], s5.at[t, pl.ds(2 * y, 2)], peer_r[0])
        yield
        copy.wait_recv()
        keeps.append(pltpu.make_async_copy(s5.at[t], gf_ref.at[t], keep_sem.at[2 * t]))
        keeps[-1].start()
        numbers = (3, 4) if t == 3 else (t,)
        for number in numbers:
            for k in range(3):
                loads[5 * k + number].wait()
        for p in range(4):
            for col, number, r0, c0, nr, nc in places(t, p):
                where = (slice(r0, r0 + nr), slice(c0, c0 + nc))
                m, v, w = (held[5 * k + number][where] for k in range(3))
                grad = s5[t, p, :, col : col + nc].astype(F32) / total
                up[t, p, :, col : col + nc] = adam(grad, m, v, w, RATES[number], True)[2].astype(BF16)
        copy = send(up.at[t], u_ref.at[t, shard], peer_x)
        keeps.append(pltpu.make_async_copy(up.at[t], u_ref.at[t, shard], keep_sem.at[2 * t + 1]))
        keeps[-1].start()
        one = send(up.at[t], u_ref.at[t, shard], peer_c)
        yield
        copy.wait_recv()
        other = flip(shard, 1)
        two = send(u_ref.at[t, other], u_ref.at[t, other], peer_c)
        yield
        one.wait_recv()
        two.wait_recv()

    flows = [gain_flow()] + [flow(t) for t in range(4)]
    offsets = [0, 0, 1, 2, 3]
    slot = 0
    live = set(range(5))
    while live:
        for k in range(5):
            if k in live and slot >= offsets[k]:
                try:
                    next(flows[k])
                except StopIteration:
                    live.discard(k)
        slot += 1
    for copy in sent:
        copy.wait_send()
    for copy in keeps:
        copy.wait()


def run_exchange(mesh_shape, rows, gr, gains, state, gain_state):
    bits = mesh_shape["rep"].bit_length() - 1
    total = float(rows * mesh_shape["rep"] * mesh_shape["shard"])
    vm = pl.BlockSpec(memory_space=pltpu.VMEM)
    hbm = pl.BlockSpec(memory_space=pl.ANY)
    sd = jax.ShapeDtypeStruct
    copies = 4 * (9 + bits) + (bits + 2) + 3 + 8
    npeer = bits + 2
    return pl.pallas_call(
        lambda *refs: exchange_kernel(bits, total, *refs),
        name="exchange",
        out_shape=(
            sd((4, 4, PR, PC), BF16),
            sd((4, 4, 4, PR, PC), BF16),
            sd((4, 8, PR), F32),
            sd((4, 8, PR), F32),
        ),
        in_specs=[vm, vm] + [hbm] * 15 + [vm] * 6,
        out_specs=(hbm, hbm, vm, vm),
        scratch_shapes=[
            pltpu.VMEM((4, 2, 4, PR, PC), BF16),
            pltpu.VMEM((4, 2, 4, PR, PC), BF16),
            pltpu.VMEM((4, 4, SPLIT, PC), BF16),
            pltpu.VMEM((4, 4, SPLIT, PC), BF16),
            pltpu.VMEM((4, 2, 2, PR - SPLIT, PC), BF16),
            pltpu.VMEM((4, 2, 2, PR - SPLIT, PC), BF16),
            pltpu.VMEM((4, 2, PR, PC), BF16),
            pltpu.VMEM((4, 2, PR, PC), BF16),
            pltpu.VMEM((4, bits - 1, PR, PC), BF16),
            pltpu.VMEM((4, PR, PC), BF16),
            pltpu.VMEM((4, bits - 2, PR, PC), BF16),
            pltpu.VMEM((4, 4, PR, PC), BF16),
            pltpu.VMEM((4, 4, PR, PC), BF16),
            pltpu.VMEM((npeer, 4, 8, PR), F32),
            pltpu.VMEM((npeer, 4, 8, PR), F32),
            pltpu.VMEM((4, 8, PR), F32),
        ]
        + [pltpu.VMEM(a.shape, F32) for a in state]
        + [
            pltpu.SemaphoreType.DMA((copies,)),
            pltpu.SemaphoreType.DMA((copies,)),
            pltpu.SemaphoreType.DMA((15,)),
            pltpu.SemaphoreType.DMA((8,)),
        ],
        compiler_params=pltpu.CompilerParams(
            vmem_limit_bytes=62 * 2**20, collective_id=0, has_side_effects=True
        ),
    )(gr, gains, *state, *gain_state)


def update_kernel(total, *refs):
    gf_ref, u_ref, gsum_ref = refs[:3]
    state = refs[3:18]
    gain_state = refs[18:24]
    outs = refs[24:44]
    gain_outs = refs[44:52]
    rounded = refs[52:57]
    low, sem = refs[57:]
    copies = []
    for t in range(3):
        for s in range(4):
            for p in range(4):
                a, b = (s, p) if t < 2 else (p, s)
                dst = rounded[t].at[pl.ds(a * PR, PR), pl.ds(b * PC, PC)]
                copies.append(pltpu.make_async_copy(u_ref.at[t, s, p], dst, sem.at[len(copies)]))
    copies.append(pltpu.make_async_copy(u_ref.at[3], low, sem.at[len(copies)]))
    for copy in copies:
        copy.start()
    shard = lax.axis_index("shard")
    grad = gsum_ref[shard] / total
    for k in range(2):
        m, v, w = (gain_state[2 * q + k][...].reshape(1, PR) for q in range(3))
        one = grad[k : k + 1]
        velocity, spread, updated = adam(one, m, v, w, BASE_RATE, False)
        for q, value in enumerate((one, updated, velocity, spread)):
            gain_outs[2 * q + k][...] = value.reshape(PR)
    for t in range(4):
        for p in range(4):
            for col, number, r0, c0, nr, nc in places(t, p):
                where = (slice(r0, r0 + nr), slice(c0, c0 + nc))
                m, v, w = (state[5 * k + number][where] for k in range(3))
                grad = gf_ref[t, p, :, col : col + nc].astype(F32) / total
                velocity, spread, updated = adam(grad, m, v, w, RATES[number], True)
                for q, value in enumerate((grad, updated, velocity, spread)):
                    outs[5 * q + number][where] = value
    copies[-1].wait()
    for s in range(4):
        for p in range(4):
            for col, number, r0, c0, nr, nc in places(3, p):
                rounded[number][s * PR : (s + 1) * PR, c0 : c0 + nc] = low[s, p, :, col : col + nc]
    for copy in copies[:-1]:
        copy.wait()


def run_update(total, gf, u, gsum, state, gain_state):
    vm = pl.BlockSpec(memory_space=pltpu.VMEM)
    hbm = pl.BlockSpec(memory_space=pl.ANY)
    sd = jax.ShapeDtypeStruct
    shapes = [a.shape for a in state[:5]]
    return pl.pallas_call(
        lambda *refs: update_kernel(total, *refs),
        name="update",
        out_shape=tuple(sd(s, F32) for s in shapes * 4)
        + (sd((PR,), F32),) * 8
        + (sd((D, FF), BF16),) * 3
        + (sd((D, QKV), BF16), sd((D, D), BF16)),
        in_specs=[vm, hbm, vm] + [vm] * 21,
        out_specs=(vm,) * 28 + (hbm,) * 3 + (vm,) * 2,
        scratch_shapes=[pltpu.VMEM((4, 4, PR, PC), BF16), pltpu.SemaphoreType.DMA((49,))],
        compiler_params=pltpu.CompilerParams(vmem_limit_bytes=62 * 2**20),
    )(gf, u, gsum, *state, *gain_state)


def solution(mesh):
    mesh_shape = dict(mesh.shape)

    def body(
        tokens, cotangent, segment_ids, current_attention, current_project, current_output,
        current_feeding, current_gating, current_upward, current_downward, *state_all,
    ):
        rows = tokens.shape[0]
        total = float(rows * mesh_shape["rep"] * mesh_shape["shard"])
        state, gain_state = [], []
        for k in range(3):
            at, pr, ou, fe, ga, uw, dw = state_all[7 * k : 7 * k + 7]
            state += [ga, uw, dw.T, pr, ou]
            gain_state += [at, fe]
        bot, tgt, gains, gr = run_block(
            tokens.T, cotangent.T, segment_ids, current_attention, current_feeding,
            current_project, current_output, current_gating, current_upward, current_downward.T,
        )
        gf, u, gsum, gup = run_exchange(mesh_shape, rows, gr, gains, state, gain_state)
        out = run_update(total, gf, u, gsum, state, gain_state)
        results = [bot.T, tgt.T]
        for q in range(4):
            ga, uw, dw, pr, ou = out[5 * q : 5 * q + 5]
            at, fe = out[20 + 2 * q : 22 + 2 * q]
            results += [at, pr, ou, fe, ga, uw, dw.T]
        ga, uw, dw, pr, ou = out[28:33]
        at, fe = (gup[:, k].reshape(D).astype(BF16) for k in range(2))
        return (*results, at, pr, ou, fe, ga, uw, dw.T)

    row, vec = P("shard", None), P("shard")
    seven = (vec, row, row, vec, row, row, row)
    spread = P(("shard", "rep"), None)
    in_specs = (spread, spread, P(("shard", "rep"))) + (P(),) * 7 + seven * 3
    out_specs = (spread, spread) + seven * 4 + (P(),) * 7
    return jax.shard_map(body, mesh=mesh, in_specs=in_specs, out_specs=out_specs, check_vma=False)
```

```python
import math

import jax
import jax.numpy as jnp
from jax import lax
from jax.experimental import pallas as pl
from jax.experimental.pallas import tpu as pltpu
from jax.sharding import PartitionSpec as P

D = 576
H = 9
KV = 3
HS = 64
FF = 1536
QKV = 960
STEP = 5
GROUP = H // KV

EPSILON = 1e-05
THETA = 10000.0
BETA = 0.5
ADAM_EPSILON = 1e-08
DECAY = 0.1
NEGATIVE = -1e30
BASE_RATE = 0.3

F32 = jnp.float32
BF16 = jnp.bfloat16
T = 256
PR = D // 4
PC = FF // 4


def dot(a, b):
    return jnp.dot(a, b, preferred_element_type=F32)


def dot_t(a, b):
    return lax.dot_general(a, b, (((1,), (1,)), ((), ())), preferred_element_type=F32)


def column(ref, size):
    row = jnp.broadcast_to(ref[...].astype(F32).reshape(1, size), (8, size))
    return row.T[:, :1]


def block_kernel(
    xt_ref, ct_ref, seg_ref, g1_ref, g2_ref, wp_ref, wo_ref, wg_ref, wu_ref, wdt_ref,
    bot_ref, tgt_ref, gain_ref, gr_ref,
    qt, kt_, vt, kn, vn, nt, mt, gmt, et, eb, invl, gres, dgain,
):
    rows = xt_ref.shape[1]
    tiles = rows // T
    half = HS // 2

    seg_row = seg_ref[...].astype(F32)
    seg_cols = jnp.broadcast_to(seg_row, (8, rows)).T[:, :1]
    starts = jnp.zeros((1, rows), F32)
    for k in range(0, rows, 128):
        lower = (seg_cols[k : k + 128] < seg_row).astype(F32)
        starts = starts + jnp.sum(lower, axis=0, keepdims=True)
    places_row = lax.broadcasted_iota(jnp.int32, (1, rows), 1).astype(F32)
    index = lax.broadcasted_iota(jnp.int32, (half, 1), 0).astype(F32)
    frequency = jnp.exp(index * (-2.0 * math.log(THETA) / HS))
    angles = frequency * (places_row - starts)
    cosine = jnp.cos(angles)
    sine = jnp.sin(angles)

    gain1 = column(g1_ref, D)
    gain2 = column(g2_ref, D)
    dgain[...] = jnp.zeros_like(dgain)

    def unit_one(cols):
        xf = xt_ref[:, cols].astype(F32)
        scale = lax.rsqrt(jnp.mean(xf * xf, axis=0, keepdims=True) + EPSILON)
        return xf * scale, scale

    def project(wpt):
        wpt[...] = wp_ref[...].T
        for r in range(tiles):
            r0 = r * T
            cs = cosine[:, r0 : r0 + T]
            sn = sine[:, r0 : r0 + T]
            unit, _ = unit_one(slice(r0, r0 + T))
            normed = (unit * gain1).astype(BF16)
            nt[:, r0 : r0 + T] = normed
            joined = dot(wpt[...], normed)
            for h in range(H + 2 * KV):
                jt = joined[h * HS : (h + 1) * HS]
                a = jt[:half]
                b = jt[half:]
                if h < H:
                    qt[h, 0:half, r0 : r0 + T] = ((a * cs - b * sn) * (HS**-0.5)).astype(BF16)
                    qt[h, half:HS, r0 : r0 + T] = ((b * cs + a * sn) * (HS**-0.5)).astype(BF16)
                elif h < H + KV:
                    kt_[h - H, 0:half, r0 : r0 + T] = (a * cs - b * sn).astype(BF16)
                    kt_[h - H, half:HS, r0 : r0 + T] = (b * cs + a * sn).astype(BF16)
                else:
                    vt[h - H - KV, :, r0 : r0 + T] = jt.astype(BF16)

    pl.run_scoped(project, pltpu.VMEM((QKV, D), BF16))
    for n in range(KV):
        kn[n] = kt_[n].T
        vn[n] = vt[n].T

    def ef(k, i):
        if k < 2:
            return et, k * T, i * T
        return eb, (k - 2) * T, (i - 2) * T

    def forward(bias, sc):
        for i in range(tiles):
            for k in range(i + 1):
                kk = lax.broadcasted_iota(jnp.int32, (T, T), 0).astype(F32) + float(k * T)
                ok = kk >= starts[:, i * T : (i + 1) * T]
                if k == i:
                    qq = lax.broadcasted_iota(jnp.int32, (T, T), 1).astype(F32) + float(i * T)
                    ok = ok & (kk <= qq)
                bias[i * (i + 1) // 2 + k] = jnp.where(ok, 0.0, NEGATIVE)

        def head(h, _):
            n = h // GROUP
            for i in range(tiles):
                q = qt[h, :, i * T : (i + 1) * T]
                peak = None
                for k in range(i + 1):
                    s = dot(kn[n, k * T : (k + 1) * T, :], q) + bias[i * (i + 1) // 2 + k]
                    sc[i % 2, k] = s
                    top = jnp.max(s, axis=0, keepdims=True)
                    peak = top if peak is None else jnp.maximum(peak, top)
                total = jnp.zeros((1, T), F32)
                out = jnp.zeros((HS, T), F32)
                for k in range(i + 1):
                    e = jnp.exp(sc[i % 2, k] - peak)
                    total = total + jnp.sum(e, axis=0, keepdims=True)
                    e16 = e.astype(BF16)
                    ref, a, b = ef(k, i)
                    ref[h, a : a + T, b : b + T] = e16
                    out = out + dot(vt[n, :, k * T : (k + 1) * T], e16)
                inverse = 1.0 / total
                invl[h, :, i * T : (i + 1) * T] = inverse
                mt[pl.ds(pl.multiple_of(h * HS, HS), HS), i * T : (i + 1) * T] = (
                    out * inverse
                ).astype(BF16)
            return 0

        lax.fori_loop(0, H, head, 0)

    pl.run_scoped(
        forward,
        pltpu.VMEM((tiles * (tiles + 1) // 2, T, T), F32),
        pltpu.VMEM((2, tiles, T, T), F32),
    )

    RT = 512
    CT = 256

    def feeding(wot, cn, n2, n2t, hid, gg, gu, res):
        wot[...] = wo_ref[...].T
        cn[...] = ct_ref[...].T

        def rowtile(r, _):
            rs = pl.ds(pl.multiple_of(r * RT, RT), RT)
            residual = xt_ref[:, rs].astype(F32) + dot(wot[...], mt[:, rs])
            scale = lax.rsqrt(jnp.mean(residual * residual, axis=0, keepdims=True) + EPSILON)
            res[...] = residual
            n2v = (residual * scale * gain2).astype(BF16)
            n2t[:, rs] = n2v
            n2[...] = n2v.T

            def col(j, _):
                js = pl.ds(pl.multiple_of(j * CT, CT), CT)
                gate = dot(n2[...], wg_ref[:, js])
                up = dot(n2[...], wu_ref[:, js])
                gh = dot(cn[rs, :], wdt_ref[:, js])
                sg = 0.5 * jnp.tanh(0.5 * gate) + 0.5
                sl = gate * sg
                hid[rs, js] = (sl * up).astype(BF16)
                gg[rs, js] = (gh * up * (sg + sl * (1.0 - sg))).astype(BF16)
                gu[rs, js] = (gh * sl).astype(BF16)
                return 0

            lax.fori_loop(0, FF // CT, col, 0)
            residual = res[...]
            bot_ref[:, rs] = (residual + dot_t(wdt_ref[...], hid[rs, :])).astype(BF16)
            gn2 = dot_t(wg_ref[...], gg[rs, :]) + dot_t(wu_ref[...], gu[rs, :])
            unit = residual * scale
            dgain[:, 1:2] += jnp.sum(gn2 * unit, axis=1, keepdims=True)
            e = gn2 * gain2
            gr = ct_ref[:, rs].astype(F32) + scale * (
                e - unit * jnp.mean(e * unit, axis=0, keepdims=True)
            )
            gres[:, rs] = gr
            gmt[:, rs] = dot(wo_ref[...], gr.astype(BF16)).astype(BF16)
            return 0

        lax.fori_loop(0, rows // RT, rowtile, 0)

        def wide(j, _):
            js = pl.ds(pl.multiple_of(j * PC, PC), PC)
            gr_ref[2, j] = dot(ct_ref[...], hid[:, js]).astype(BF16).reshape(4, PR, PC)
            gr_ref[0, :, j] = dot(n2t[...], gg[:, js]).astype(BF16).reshape(4, PR, PC)
            gr_ref[1, :, j] = dot(n2t[...], gu[:, js]).astype(BF16).reshape(4, PR, PC)
            return 0

        lax.fori_loop(0, FF // PC, wide, 0)
        gr_ref[3, :, 3] = dot_t(mt[...], gres[:PC].astype(BF16)).astype(BF16).reshape(4, PR, PC)
        part = dot_t(mt[...], gres[PC:].astype(BF16)).astype(BF16)
        gr_ref[3, :, 2, :, PC // 2 :] = part.reshape(4, PR, PC // 2)

    pl.run_scoped(
        feeding,
        pltpu.VMEM((D, D), BF16),
        pltpu.VMEM((rows, D), BF16),
        pltpu.VMEM((RT, D), BF16),
        pltpu.VMEM((D, rows), BF16),
        pltpu.VMEM((rows, FF), BF16),
        pltpu.VMEM((rows, FF), BF16),
        pltpu.VMEM((rows, FF), BF16),
        pltpu.VMEM((D, RT), F32),
    )

    def backward(ds, gjt, dk, dv, cs_ref, sn_ref):
        cs_ref[...] = cosine
        sn_ref[...] = sine

        def unrotate(v, base):
            a = v[:half]
            b = v[half:]
            cs = cs_ref[...]
            sn = sn_ref[...]
            gjt[pl.ds(pl.multiple_of(base, HS), half), :] = (a * cs + b * sn).astype(BF16)
            gjt[pl.ds(pl.multiple_of(base + half, half), half), :] = (b * cs - a * sn).astype(BF16)

        def head(h, _):
            n = h // GROUP
            hs = pl.ds(pl.multiple_of(h * HS, HS), HS)
            first = lax.rem(h, GROUP) == 0

            @pl.when(first)
            def _():
                dk[...] = jnp.zeros_like(dk)
                dv[...] = jnp.zeros_like(dv)

            do = (gmt[hs, :].astype(F32) * invl[h]).astype(BF16)
            delta = jnp.sum(do.astype(F32) * mt[hs, :].astype(F32), axis=0, keepdims=True)
            for k in range(tiles):
                ks = slice(k * T, (k + 1) * T)
                for i in range(k, tiles):
                    cols = slice(i * T, (i + 1) * T)
                    ref, a, b = ef(k, i)
                    dp = dot(vn[n, ks, :], do[:, cols]) - delta[:, cols]
                    ds[ks, cols] = (ref[h, a : a + T, b : b + T].astype(F32) * dp).astype(BF16)
                ref, a, b = ef(k, k)
                dv[ks, :] += dot_t(ref[h, a : a + T, b : b + rows - k * T], do[:, k * T :])
                dk[ks, :] += dot_t(ds[ks, k * T :], qt[h, :, k * T :])
            dq = [
                dot(kt_[n, :, : (i + 1) * T], ds[: (i + 1) * T, i * T : (i + 1) * T])
                for i in range(tiles)
            ]
            unrotate(jnp.concatenate(dq, axis=1) * (HS**-0.5), h * HS)

            @pl.when(lax.rem(h, GROUP) == GROUP - 1)
            def _():
                unrotate(dk[...].T, H * HS + n * HS)
                gjt[pl.ds(pl.multiple_of((H + KV + n) * HS, HS), HS), :] = dv[...].T.astype(BF16)

            return 0

        lax.fori_loop(0, H, head, 0)

        for p in range(2):
            part = dot_t(nt[...], gjt[p * PC : (p + 1) * PC, :]).astype(BF16)
            gr_ref[3, :, p] = part.reshape(4, PR, PC)
        part = dot_t(nt[...], gjt[2 * PC :, :]).astype(BF16)
        gr_ref[3, :, 2, :, : PC // 2] = part.reshape(4, PR, PC // 2)

        def rowtile(r, _):
            rs = pl.ds(pl.multiple_of(r * T, T), T)
            gn = dot(wp_ref[...], gjt[:, rs])
            unit, scale = unit_one(rs)
            dgain[:, 0:1] += jnp.sum(gn * unit, axis=1, keepdims=True)
            e = gn * gain1
            tg = gres[:, rs] + scale * (e - unit * jnp.mean(e * unit, axis=0, keepdims=True))
            tgt_ref[:, rs] = tg.astype(BF16)
            return 0

        lax.fori_loop(0, rows // T, rowtile, 0)
        for s in range(4):
            gain_ref[s] = dgain[s * PR : (s + 1) * PR, :].T

    pl.run_scoped(
        backward,
        pltpu.VMEM((rows, rows), BF16),
        pltpu.VMEM((QKV, rows), BF16),
        pltpu.VMEM((rows, HS), F32),
        pltpu.VMEM((rows, HS), F32),
        pltpu.VMEM((half, rows), F32),
        pltpu.VMEM((half, rows), F32),
    )


def run_block(xt, ct, seg, g1, g2, wp, wo, wg, wu, wdt):
    rows = xt.shape[1]
    vm = pl.BlockSpec(memory_space=pltpu.VMEM)
    sd = jax.ShapeDtypeStruct
    return pl.pallas_call(
        block_kernel,
        name="block",
        out_shape=(
            sd((D, rows), BF16),
            sd((D, rows), BF16),
            sd((4, 8, PR), F32),
            sd((4, 4, 4, PR, PC), BF16),
        ),
        in_specs=[vm] * 10,
        out_specs=(vm,) * 4,
        scratch_shapes=[
            pltpu.VMEM((H, HS, rows), BF16),
            pltpu.VMEM((KV, HS, rows), BF16),
            pltpu.VMEM((KV, HS, rows), BF16),
            pltpu.VMEM((KV, rows, HS), BF16),
            pltpu.VMEM((KV, rows, HS), BF16),
            pltpu.VMEM((D, rows), BF16),
            pltpu.VMEM((D, rows), BF16),
            pltpu.VMEM((D, rows), BF16),
            pltpu.VMEM((H, 2 * T, rows), BF16),
            pltpu.VMEM((H, 2 * T, rows - 2 * T), BF16),
            pltpu.VMEM((H, 1, rows), F32),
            pltpu.VMEM((D, rows), F32),
            pltpu.VMEM((D, 8), F32),
        ],
        compiler_params=pltpu.CompilerParams(vmem_limit_bytes=62 * 2**20),
    )(xt, ct, seg.reshape(1, rows), g1, g2, wp, wo, wg, wu, wdt)
MESH = pl.DeviceIdType.MESH
SPLIT = 80
RATES = tuple(
    BASE_RATE * v
    for v in (float(D) ** -0.5, float(D) ** -0.5, float(FF) ** -0.5, float(D) ** -0.5, float(max(D // 96, 1)) ** -0.5)
)
CORRECTION = 1.0 - BETA**STEP


def adam(grad, master, moment, variance, rate, decay):
    velocity = BETA * moment + (1.0 - BETA) * grad
    spread = BETA * variance + (1.0 - BETA) * grad * grad
    direction = velocity / CORRECTION / (jnp.sqrt(spread / CORRECTION) + ADAM_EPSILON)
    if decay:
        direction = direction + DECAY * master
    return velocity, spread, master - rate * direction


def places(t, p):
    if t < 2:
        return [(0, t, 0, p * PC, PR, PC)]
    if t == 2:
        return [(0, 2, p * PR, 0, PR, PC)]
    if p < 2:
        return [(0, 3, 0, p * PC, PR, PC)]
    if p == 2:
        return [(0, 3, 0, 2 * PC, PR, PC // 2), (PC // 2, 4, 0, PC, PR, PC // 2)]
    return [(0, 4, 0, 0, PR, PC)]


def add_into(dst, a, b):
    dst[...] = (a[...].astype(F32) + b[...].astype(F32)).astype(BF16)


def exchange_kernel(bits, total, *refs):
    gr_ref, gain_ref = refs[:2]
    state = refs[2:17]
    gain_state = refs[17:23]
    gf_ref, u_ref, gsum_ref, gup_ref = refs[23:27]
    (s1, r1, s2a, r2a, s2b, r2b, s3, r3, s4, r4, r5, s5, up, gs, grc, gu) = refs[27:43]
    held = refs[43:58]
    send_sem, recv_sem, load_sem, keep_sem = refs[58:62]

    shard = lax.axis_index("shard")
    rep = lax.axis_index("rep")
    x, core = shard // 2, lax.rem(shard, 2)
    y, zl = lax.rem(rep, 2), lax.rem(rep // 2, 2)

    def flip(index, bit):
        size = 1 << bit
        return index + size - 2 * size * lax.rem(index // size, 2)

    peer_c = (flip(shard, 0), rep)
    peer_x = (flip(shard, 1), rep)
    peer_r = [(shard, flip(rep, b)) for b in range(bits)]
    peers = [peer_c, peer_x] + peer_r

    loads = []
    for number in range(15):
        loads.append(pltpu.make_async_copy(state[number], held[number], load_sem.at[number]))
        loads[-1].start()

    barrier = pltpu.get_barrier_semaphore()
    for peer in peers:
        pl.semaphore_signal(barrier, inc=1, device_id=peer, device_id_type=MESH)
    pl.semaphore_wait(barrier, len(peers))

    sent = []

    def send(src, dst, peer):
        n = len(sent)
        copy = pltpu.make_async_remote_copy(
            src_ref=src, dst_ref=dst, send_sem=send_sem.at[n], recv_sem=recv_sem.at[n],
            device_id=peer, device_id_type=MESH,
        )
        copy.start()
        sent.append(copy)
        return copy

    keeps = []

    def gain_flow():
        copy = send(gain_ref, grc.at[0], peer_c)
        yield
        for b, peer in enumerate(peers):
            copy.wait_recv()
            gs[b] = (gain_ref[...] if b == 0 else gs[b - 1]) + grc[b]
            if b + 1 < len(peers):
                copy = send(gs.at[b], grc.at[b + 1], peers[b + 1])
                yield
        gsum_ref[...] = gs[len(peers) - 1]
        grad = gs[len(peers) - 1, shard] / total
        for k in range(2):
            m, v, w = (gain_state[2 * q + k][...].reshape(1, PR) for q in range(3))
            gu[shard, k : k + 1, :] = adam(grad[k : k + 1], m, v, w, BASE_RATE, False)[2]
        copy = send(gu.at[shard], gu.at[shard], peer_x)
        yield
        copy.wait_recv()
        one = send(gu.at[shard], gu.at[shard], peer_c)
        two = send(gu.at[flip(shard, 1)], gu.at[flip(shard, 1)], peer_c)
        yield
        one.wait_recv()
        two.wait_recv()
        gup_ref[...] = gu[...]

    def flow(t):
        copies = [
            send(gr_ref.at[t, 2 * i + 1 - core], r1.at[t, i], peer_c) for i in range(2)
        ]
        yield
        for copy in copies:
            copy.wait_recv()
        for i in range(2):
            def step(p, _):
                add_into(s1.at[t, i, p], gr_ref.at[t, 2 * i + core, p], r1.at[t, i, p])
                return 0

            lax.fori_loop(0, 4, step, 0)
        a, b = pl.ds(0, SPLIT), pl.ds(SPLIT, PR - SPLIT)
        one = send(s1.at[t, 1 - x, :, a], r2a.at[t], peer_x)
        two = send(s1.at[t, :, pl.ds(2 * (1 - y), 2), b], r2b.at[t], peer_r[0])
        yield
        one.wait_recv()
        two.wait_recv()
        for p in range(4):
            add_into(s2a.at[t, p], s1.at[t, x, p, a], r2a.at[t, p])
        for i in range(2):
            for q in range(2):
                add_into(s2b.at[t, i, q], s1.at[t, i, 2 * y + q, b], r2b.at[t, i, q])
        one = send(s2a.at[t, pl.ds(2 * (1 - y), 2)], r3.at[t, :, a], peer_r[0])
        two = send(s2b.at[t, 1 - x], r3.at[t, :, b], peer_x)
        yield
        one.wait_recv()
        two.wait_recv()
        for q in range(2):
            add_into(s3.at[t, q, a], s2a.at[t, 2 * y + q], r3.at[t, q, a])
            add_into(s3.at[t, q, b], s2b.at[t, x, q], r3.at[t, q, b])
        copy = send(s3.at[t, 1 - zl], r4.at[t], peer_r[1])
        yield
        copy.wait_recv()
        add_into(s4.at[t, 0], s3.at[t, zl], r4.at[t])
        for k in range(bits - 2):
            copy = send(s4.at[t, k], r5.at[t, k], peer_r[2 + k])
            yield
            copy.wait_recv()
            add_into(s4.at[t, k + 1], s4.at[t, k], r5.at[t, k])
        mine = 2 * y + zl
        s5[t, mine] = s4[t, bits - 2]
        copy = send(s4.at[t, bits - 2], s5.at[t, mine], peer_r[1])
        yield
        copy.wait_recv()
        copy = send(s5.at[t, pl.ds(2 * y, 2)], s5.at[t, pl.ds(2 * y, 2)], peer_r[0])
        yield
        copy.wait_recv()
        keeps.append(pltpu.make_async_copy(s5.at[t], gf_ref.at[t], keep_sem.at[2 * t]))
        keeps[-1].start()
        numbers = (3, 4) if t == 3 else (t,)
        for number in numbers:
            for k in range(3):
                loads[5 * k + number].wait()
        for p in range(4):
            for col, number, r0, c0, nr, nc in places(t, p):
                where = (slice(r0, r0 + nr), slice(c0, c0 + nc))
                m, v, w = (held[5 * k + number][where] for k in range(3))
                grad = s5[t, p, :, col : col + nc].astype(F32) / total
                up[t, p, :, col : col + nc] = adam(grad, m, v, w, RATES[number], True)[2].astype(BF16)
        copy = send(up.at[t], u_ref.at[t, shard], peer_x)
        one = send(up.at[t], u_ref.at[t, shard], peer_c)
        u_ref[t, shard] = up[t]
        yield
        copy.wait_recv()
        other = flip(shard, 1)
        two = send(u_ref.at[t, other], u_ref.at[t, other], peer_c)
        yield
        one.wait_recv()
        two.wait_recv()

    flows = [gain_flow()] + [flow(t) for t in range(4)]
    offsets = [0, 0, 1, 2, 3]
    slot = 0
    live = set(range(5))
    while live:
        for k in range(5):
            if k in live and slot >= offsets[k]:
                try:
                    next(flows[k])
                except StopIteration:
                    live.discard(k)
        slot += 1
    for copy in sent:
        copy.wait_send()
    for copy in keeps:
        copy.wait()


def run_exchange(mesh_shape, rows, gr, gains, state, gain_state):
    bits = mesh_shape["rep"].bit_length() - 1
    total = float(rows * mesh_shape["rep"] * mesh_shape["shard"])
    vm = pl.BlockSpec(memory_space=pltpu.VMEM)
    hbm = pl.BlockSpec(memory_space=pl.ANY)
    sd = jax.ShapeDtypeStruct
    copies = 4 * (9 + bits) + (bits + 2) + 3 + 8
    npeer = bits + 2
    return pl.pallas_call(
        lambda *refs: exchange_kernel(bits, total, *refs),
        name="exchange",
        out_shape=(
            sd((4, 4, PR, PC), BF16),
            sd((4, 4, 4, PR, PC), BF16),
            sd((4, 8, PR), F32),
            sd((4, 8, PR), F32),
        ),
        in_specs=[vm, vm] + [hbm] * 15 + [vm] * 6,
        out_specs=(hbm, vm, vm, vm),
        scratch_shapes=[
            pltpu.VMEM((4, 2, 4, PR, PC), BF16),
            pltpu.VMEM((4, 2, 4, PR, PC), BF16),
            pltpu.VMEM((4, 4, SPLIT, PC), BF16),
            pltpu.VMEM((4, 4, SPLIT, PC), BF16),
            pltpu.VMEM((4, 2, 2, PR - SPLIT, PC), BF16),
            pltpu.VMEM((4, 2, 2, PR - SPLIT, PC), BF16),
            pltpu.VMEM((4, 2, PR, PC), BF16),
            pltpu.VMEM((4, 2, PR, PC), BF16),
            pltpu.VMEM((4, bits - 1, PR, PC), BF16),
            pltpu.VMEM((4, PR, PC), BF16),
            pltpu.VMEM((4, bits - 2, PR, PC), BF16),
            pltpu.VMEM((4, 4, PR, PC), BF16),
            pltpu.VMEM((4, 4, PR, PC), BF16),
            pltpu.VMEM((npeer, 4, 8, PR), F32),
            pltpu.VMEM((npeer, 4, 8, PR), F32),
            pltpu.VMEM((4, 8, PR), F32),
        ]
        + [pltpu.VMEM(a.shape, F32) for a in state]
        + [
            pltpu.SemaphoreType.DMA((copies,)),
            pltpu.SemaphoreType.DMA((copies,)),
            pltpu.SemaphoreType.DMA((15,)),
            pltpu.SemaphoreType.DMA((8,)),
        ],
        compiler_params=pltpu.CompilerParams(
            vmem_limit_bytes=62 * 2**20, collective_id=0, has_side_effects=True
        ),
    )(gr, gains, *state, *gain_state)


def update_kernel(total, *refs):
    gf_ref, u_ref, gsum_ref = refs[:3]
    state = refs[3:18]
    gain_state = refs[18:24]
    outs = refs[24:44]
    gain_outs = refs[44:52]
    rounded = refs[52:57]
    gf, low = refs[57:59]
    held = refs[59:74]
    made = refs[74:94]
    wide = refs[94:99]
    load_sem, low_sem, gf_sem, out_sem, wide_sem = refs[99:]

    order = (0, 1, 2, 3, 4)
    loads = {}
    grads = []
    for t in range(4):
        grads.append(pltpu.make_async_copy(gf_ref.at[t], gf.at[t], gf_sem.at[t]))
        grads[-1].start()
        for number in ((t,) if t < 3 else (3, 4)):
            for k in range(3):
                n = 5 * k + number
                loads[n] = pltpu.make_async_copy(state[n], held[n], load_sem.at[n])
                loads[n].start()
    lows = []
    for t in range(4):
        lows.append(pltpu.make_async_copy(u_ref.at[t], low.at[t], low_sem.at[t]))
        lows[-1].start()
    stores = []

    def store(src, dst, sem):
        stores.append(pltpu.make_async_copy(src, dst, sem))
        stores[-1].start()

    shard = lax.axis_index("shard")
    grad = gsum_ref[shard] / total
    for k in range(2):
        m, v, w = (gain_state[2 * q + k][...].reshape(1, PR) for q in range(3))
        one = grad[k : k + 1]
        velocity, spread, updated = adam(one, m, v, w, BASE_RATE, False)
        for q, value in enumerate((one, updated, velocity, spread)):
            gain_outs[2 * q + k][...] = value.reshape(PR)
    for t in range(4):
        numbers = (t,) if t < 3 else (3, 4)
        grads[t].wait()
        for number in numbers:
            for k in range(3):
                loads[5 * k + number].wait()
        for p in range(4):
            for col, number, r0, c0, nr, nc in places(t, p):
                where = (slice(r0, r0 + nr), slice(c0, c0 + nc))
                m, v, w = (held[5 * k + number][where] for k in range(3))
                grad = gf[t, p, :, col : col + nc].astype(F32) / total
                velocity, spread, updated = adam(grad, m, v, w, RATES[number], True)
                for q, value in enumerate((grad, updated, velocity, spread)):
                    made[5 * q + number][where] = value
        for number in numbers:
            for q in range(4):
                n = 5 * q + number
                store(made[n], outs[n], out_sem.at[n])
        lows[t].wait()
        for s in range(4):
            for p in range(4):
                if t == 2:
                    wide[2][p * PR : (p + 1) * PR, s * PC : (s + 1) * PC] = low[2, s, p]
                    continue
                for col, number, r0, c0, nr, nc in places(t, p):
                    wide[number][s * PR : (s + 1) * PR, c0 : c0 + nc] = low[t, s, p, :, col : col + nc]
        for number in numbers:
            store(wide[number], rounded[number], wide_sem.at[number])
    for copy in stores:
        copy.wait()


def run_update(total, gf, u, gsum, state, gain_state):
    vm = pl.BlockSpec(memory_space=pltpu.VMEM)
    hbm = pl.BlockSpec(memory_space=pl.ANY)
    sd = jax.ShapeDtypeStruct
    shapes = [a.shape for a in state[:5]]
    full = [(D, FF)] * 3 + [(D, QKV), (D, D)]
    return pl.pallas_call(
        lambda *refs: update_kernel(total, *refs),
        name="update",
        out_shape=tuple(sd(s, F32) for s in shapes * 4)
        + (sd((PR,), F32),) * 8
        + tuple(sd(s, BF16) for s in full),
        in_specs=[hbm, hbm, vm] + [hbm] * 15 + [vm] * 6,
        out_specs=(hbm,) * 20 + (vm,) * 8 + (hbm,) * 5,
        scratch_shapes=[
            pltpu.VMEM((4, 4, PR, PC), BF16),
            pltpu.VMEM((4, 4, 4, PR, PC), BF16),
        ]
        + [pltpu.VMEM(s, F32) for s in shapes * 3]
        + [pltpu.VMEM(s, F32) for s in shapes * 4]
        + [pltpu.VMEM(s, BF16) for s in full]
        + [pltpu.SemaphoreType.DMA((n,)) for n in (15, 4, 4, 20, 5)],
        compiler_params=pltpu.CompilerParams(vmem_limit_bytes=62 * 2**20),
    )(gf, u, gsum, *state, *gain_state)


def solution(mesh):
    mesh_shape = dict(mesh.shape)

    def body(
        tokens, cotangent, segment_ids, current_attention, current_project, current_output,
        current_feeding, current_gating, current_upward, current_downward, *state_all,
    ):
        rows = tokens.shape[0]
        total = float(rows * mesh_shape["rep"] * mesh_shape["shard"])
        state, gain_state = [], []
        for k in range(3):
            at, pr, ou, fe, ga, uw, dw = state_all[7 * k : 7 * k + 7]
            state += [ga, uw, dw.T, pr, ou]
            gain_state += [at, fe]
        bot, tgt, gains, gr = run_block(
            tokens.T, cotangent.T, segment_ids, current_attention, current_feeding,
            current_project, current_output, current_gating, current_upward, current_downward.T,
        )
        gf, u, gsum, gup = run_exchange(mesh_shape, rows, gr, gains, state, gain_state)
        out = run_update(total, gf, u, gsum, state, gain_state)
        results = [bot.T, tgt.T]
        for q in range(4):
            ga, uw, dw, pr, ou = out[5 * q : 5 * q + 5]
            at, fe = out[20 + 2 * q : 22 + 2 * q]
            results += [at, pr, ou, fe, ga, uw, dw.T]
        ga, uw, dw, pr, ou = out[28:33]
        at, fe = (gup[:, k].reshape(D).astype(BF16) for k in range(2))
        return (*results, at, pr, ou, fe, ga, uw, dw.T)

    row, vec = P("shard", None), P("shard")
    seven = (vec, row, row, vec, row, row, row)
    spread = P(("shard", "rep"), None)
    in_specs = (spread, spread, P(("shard", "rep"))) + (P(),) * 7 + seven * 3
    out_specs = (spread, spread) + seven * 4 + (P(),) * 7
    return jax.shard_map(body, mesh=mesh, in_specs=in_specs, out_specs=out_specs, check_vma=False)
```

```python
import math

import jax
import jax.numpy as jnp
from jax import lax
from jax.experimental import pallas as pl
from jax.experimental.pallas import tpu as pltpu
from jax.sharding import PartitionSpec as P

D = 576
H = 9
KV = 3
HS = 64
FF = 1536
QKV = 960
STEP = 5
GROUP = H // KV

EPSILON = 1e-05
THETA = 10000.0
BETA = 0.5
ADAM_EPSILON = 1e-08
DECAY = 0.1
NEGATIVE = -1e30
BASE_RATE = 0.3

F32 = jnp.float32
BF16 = jnp.bfloat16
T = 256
PR = D // 4
LANES = 128
UNIT = 3 * PR
CH = 512
UNITS = 4


def dot(a, b):
    return jnp.dot(a, b, preferred_element_type=F32)


def dot_t(a, b):
    return lax.dot_general(a, b, (((1,), (1,)), ((), ())), preferred_element_type=F32)

MESH = pl.DeviceIdType.MESH
RATES = tuple(
    BASE_RATE * v
    for v in (float(D) ** -0.5, float(D) ** -0.5, float(FF) ** -0.5, float(D) ** -0.5, float(max(D // 96, 1)) ** -0.5)
)
CORRECTION = 1.0 - BETA**STEP


def blocks(u, p):
    if u < 3:
        c = p * (FF // 4) + u * LANES
        return [(0, 0, LANES, 0, 0, c), (PR, 0, LANES, 1, 0, c), (2 * PR, 0, LANES, 2, p * PR, u * LANES)]
    out = [(0, 0, LANES, 4, 0, p * LANES), (PR, 0, LANES, 3, 0, p * LANES)]
    if p < 3:
        return out + [(2 * PR, 0, LANES, 3, 0, 512 + p * LANES)]
    return out + [(2 * PR, 0, 64, 3, 0, 896), (2 * PR, 64, 64, 4, 0, 512)]


def adam(grad, master, moment, variance, rate, decay):
    velocity = BETA * moment + (1.0 - BETA) * grad
    spread = BETA * variance + (1.0 - BETA) * grad * grad
    direction = velocity / CORRECTION / (jnp.sqrt(spread / CORRECTION) + ADAM_EPSILON)
    if decay:
        direction = direction + DECAY * master
    return velocity, spread, master - rate * direction


def add_into(dst, a, b):
    dst[...] = (a[...].astype(F32) + b[...].astype(F32)).astype(BF16)


def column(ref, size):
    row = jnp.broadcast_to(ref[...].astype(F32).reshape(1, size), (8, size))
    return row.T[:, :1]


class Exchange:
    def __init__(self, bits, total, refs):
        self.__dict__.update(refs)
        self.bits, self.total = bits, total
        self.shard, self.rep = lax.axis_index("shard"), lax.axis_index("rep")
        self.x, self.core = self.shard // 2, lax.rem(self.shard, 2)
        self.y, self.zl = lax.rem(self.rep, 2), lax.rem(self.rep // 2, 2)
        self.peer_c = (self.flip(self.shard, 0), self.rep)
        self.peer_x = (self.flip(self.shard, 1), self.rep)
        self.peer_r = [(self.shard, self.flip(self.rep, b)) for b in range(bits)]
        self.peers = [self.peer_c, self.peer_x] + self.peer_r
        self.other = self.flip(self.shard, 1)
        self.not_x, self.not_core, self.not_y, self.not_zl = (1 - v for v in (self.x, self.core, self.y, self.zl))
        self.sent, self.kept, self.live = [], [], []

    @staticmethod
    def flip(index, bit):
        size = 1 << bit
        return index + size - 2 * size * lax.rem(index // size, 2)

    def greet(self):
        self.barrier = pltpu.get_barrier_semaphore()
        for peer in self.peers:
            pl.semaphore_signal(self.barrier, inc=1, device_id=peer, device_id_type=MESH)

    def met(self):
        pl.semaphore_wait(self.barrier, len(self.peers))

    def send(self, src, dst, peer):
        n = len(self.sent)

        def make():
            return pltpu.make_async_remote_copy(
                src_ref=src(), dst_ref=dst(), send_sem=self.send_sem.at[n], recv_sem=self.recv_sem.at[n],
                device_id=peer, device_id_type=MESH,
            )

        make().start()
        self.sent.append(make)
        return make

    def keep(self, src, dst):
        n = len(self.kept)

        def make():
            return pltpu.make_async_copy(src(), dst(), self.keep_sem.at[n])

        make().start()
        self.kept.append(make)

    def begin(self, flow):
        next(flow)
        self.live.append(flow)

    def tick(self):
        for flow in list(self.live):
            try:
                next(flow)
            except StopIteration:
                self.live.remove(flow)

    def finish(self):
        while self.live:
            self.tick()
        for copy in self.sent:
            copy().wait_send()
        for copy in self.kept:
            copy().wait()

    def load_state(self):
        for number, held in enumerate(self.held):
            for k in range(3):
                n = 5 * k + number
                yield pltpu.make_async_copy(self.state[n], held.at[k], self.st_sem.at[n])

    def have_state(self):
        for copy in self.load_state():
            copy.wait()
        for k in range(3):
            self.tail[k] = jnp.concatenate([self.held[3][k, :, 896:], self.held[4][k, :, 512:]], axis=1)

    def gain(self):
        gains, gs, gr, gu = self.gain_ref, self.gs, self.grc, self.gu
        copy = self.send(lambda: gains, lambda: gr.at[0], self.peers[0])
        yield
        last = len(self.peers) - 1
        for b in range(last + 1):
            copy().wait_recv()
            gs[b] = (gains[...] if b == 0 else gs[b - 1]) + gr[b]
            if b < last:
                copy = self.send(lambda b=b: gs.at[b], lambda b=b: gr.at[b + 1], self.peers[b + 1])
                yield
        self.gsum_ref[...] = gs[last]
        shard, other = self.shard, self.other
        grad = gs[last, shard] / self.total
        for k in range(2):
            m, v, w = (self.gain_state[2 * q + k][...].reshape(1, PR) for q in range(3))
            gu[shard, k : k + 1, :] = adam(grad[k : k + 1], m, v, w, BASE_RATE, False)[2]
        copy = self.send(lambda: gu.at[shard], lambda: gu.at[shard], self.peer_x)
        one = self.send(lambda: gu.at[shard], lambda: gu.at[shard], self.peer_c)
        yield
        copy().wait_recv()
        two = self.send(lambda: gu.at[other], lambda: gu.at[other], self.peer_c)
        yield
        one().wait_recv()
        two().wait_recv()
        self.gup_ref[...] = gu[...]

    def update(self, u, b, pieces):
        rs = slice(b * PR, (b + 1) * PR)

        def lanes(c):
            return pl.ds(c if isinstance(c, int) else pl.multiple_of(c, LANES), LANES)

        for py, pz in pieces:
            p = 2 * py + pz
            number = b if u < 3 else (4, 3, 3)[b]
            held, rate = self.held[number], RATES[number]
            if u < 3 and b == 2:
                r0 = p * PR if isinstance(p, int) else pl.multiple_of(p * PR, PR)
                state = [held[k, pl.ds(r0, PR), u * LANES : (u + 1) * LANES] for k in range(3)]
            elif u < 3:
                state = [held[k, :, lanes(p * (FF // 4) + u * LANES)] for k in range(3)]
            elif b < 2:
                state = [held[k, :, lanes(p * LANES)] for k in range(3)]
            else:
                if isinstance(p, int):
                    state = [self.tail[k] if p == 3 else held[k, :, lanes(512 + p * LANES)] for k in range(3)]
                else:
                    near = lanes(512 + jnp.minimum(p, 2) * LANES)
                    state = [jnp.where(p == 3, self.tail[k], held[k, :, near]) for k in range(3)]
                lane = lax.broadcasted_iota(jnp.int32, (PR, LANES), 1) + LANES * p
                rate = jnp.where(lane < QKV - 512, RATES[3], RATES[4])
            grad = self.agb[u, 2, py, pz, rs].astype(F32) / self.total
            self.agb[u, 0, py, pz, rs] = adam(grad, *state, rate, True)[2].astype(BF16)

    def unit(self, u, first, count):
        own = {"x": self.x, "y": self.y, "z": self.zl}
        far = {"x": self.not_x, "y": self.not_y, "z": self.not_zl}
        peer = {"x": self.peer_x, "y": self.peer_r[0], "z": self.peer_r[1]}
        core, not_core = self.core, self.not_core
        g, r1, s4, r5, agb = self.grads, self.r1, self.s4, self.r5, self.agb
        span = range(first, first + count)
        rs = pl.ds(first * PR, count * PR)

        def rows(b):
            return pl.ds(b * PR, PR)

        copy = self.send(lambda: g.at[u, :, not_core, :, :, rs], lambda: r1.at[u, :, :, :, rs], self.peer_c)
        yield
        copy().wait_recv()

        def both(n, _):
            i, p, q = n // 4, lax.rem(n // 2, 2), lax.rem(n, 2)
            add_into(g.at[u, i, core, p, q, rs], g.at[u, i, core, p, q, rs], r1.at[u, i, p, q, rs])
            return 0

        lax.fori_loop(0, 8, both, 0)

        def at(index):
            return (u, index["x"], core, index["y"], index["z"])

        for stage in range(3):
            landed = (self.r2, self.r3, self.r4)[stage]
            copies = []
            for b in span:
                order = HALVES[b]
                index = {d: own[d] for d in order[:stage]}
                index.update({d: slice(None) for d in order[stage + 1 :]})
                index[order[stage]] = far[order[stage]]
                free = (slice(None),) * (2 - stage)
                copies.append(self.send(
                    lambda w=at(index), b=b: g.at[w + (rows(b),)],
                    lambda f=free, b=b, landed=landed: landed.at[(u,) + f + (rows(b),)],
                    peer[order[stage]],
                ))
            yield
            for copy in copies:
                copy().wait_recv()
            for b in span:
                order = HALVES[b]
                later = sorted(order[stage + 1 :])
                for n in range(1 << len(later)):
                    index = {d: own[d] for d in order[: stage + 1]}
                    bits = tuple(n >> k & 1 for k in reversed(range(len(later))))
                    index.update(zip(later, bits))
                    w = at(index) + (rows(b),)
                    if stage < 2:
                        add_into(g.at[w], g.at[w], landed.at[(u,) + bits + (rows(b),)])
                    else:
                        add_into(s4.at[u, 0, rows(b)], g.at[w], landed.at[u, rows(b)])

        last = self.bits - 2
        for k in range(last):
            copy = self.send(lambda k=k: s4.at[u, k, rs], lambda k=k: r5.at[u, k, rs], self.peer_r[2 + k])
            yield
            copy().wait_recv()
            add_into(s4.at[u, k + 1, rs], s4.at[u, k, rs], r5.at[u, k, rs])
        y, zl = self.y, self.zl
        agb[u, 2, y, zl, rs] = s4[u, last, rs]

        for stage in range(3):
            copies = []
            for b in span:
                order = GATHERS[b]
                d = order[stage]
                known = order[:stage]
                index = (slice(None) if "y" in known else y, slice(None) if "z" in known else zl, rows(b))
                if d == "x":
                    ys = range(2) if "y" in known else (y,)
                    zs = range(2) if "z" in known else (zl,)
                    self.update(u, b, [(i, j) for i in ys for j in zs])
                    copies.append(self.send(
                        lambda w=index: agb.at[(u, 0) + w], lambda w=index: agb.at[(u, 1) + w], peer[d]
                    ))
                    continue
                kinds = pl.ds(1, 2) if "x" in known else 2
                copies.append(self.send(
                    lambda w=index, k=kinds: agb.at[(u, k) + w], lambda w=index, k=kinds: agb.at[(u, k) + w], peer[d]
                ))
            yield
            for copy in copies:
                copy().wait_recv()
        self.keep(lambda: agb.at[u, 2, :, :, rs], lambda: self.gf_ref.at[u, :, :, rs])
        for b in span:
            known = GATHERS[b][: GATHERS[b].index("x")]
            if known == "":
                self.update(u, b, [(self.not_y, zl), (y, self.not_zl), (self.not_y, self.not_zl)])
            elif known == "y":
                self.update(u, b, [(i, self.not_zl) for i in range(2)])
            elif known == "z":
                self.update(u, b, [(self.not_y, i) for i in range(2)])
        self.keep(lambda: agb.at[u, pl.ds(0, 2), :, :, rs], lambda: self.u_ref.at[u, core, :, :, :, rs])
        copy = self.send(
            lambda: agb.at[u, pl.ds(0, 2), :, :, rs], lambda: self.u_ref.at[u, core, :, :, :, rs], self.peer_c
        )
        yield
        copy().wait_recv()


HALVES = ("xyz", "yzx", "zxy")
GATHERS = ("zyx", "xzy", "yxz")


def step_kernel(bits, total, *refs):
    ins, state = refs[:10], refs[10:25]
    bot_ref, tgt_ref, gsum_ref, gup_ref, gf_ref, u_ref, e_hbm = refs[31:38]
    (
        xt_ref, ct_ref, seg_ref, g1_ref, g2_ref, wp_ref, wo_ref, wg_ref, wu_ref, wdt_ref, *gain_state,
        qt, kt_, vt, kn, vn, nt, mt, gmt, es, invl, gres, dgain, gain_ref,
        grads, r1, r2, r3, r4, s4, r5, agb, gs, grc, gu,
        send_sem, recv_sem, keep_sem, st_sem, in_sem, e_sem, out_sem,
    ) = refs[38:]
    rows = xt_ref.shape[1]
    tiles = rows // T
    half = HS // 2
    ex = Exchange(bits, total, dict(
        state=state, gain_state=gain_state, gsum_ref=gsum_ref, gup_ref=gup_ref, gf_ref=gf_ref, u_ref=u_ref,
        gain_ref=gain_ref, grads=grads, r1=r1, r2=r2, r3=r3, r4=r4, s4=s4, r5=r5, agb=agb, gs=gs, grc=grc, gu=gu,
        send_sem=send_sem, recv_sem=recv_sem, keep_sem=keep_sem, st_sem=st_sem,
    ))

    loads = [
        pltpu.make_async_copy(src, dst, in_sem.at[n])
        for n, (src, dst) in enumerate(zip(
            tuple(ins) + tuple(refs[25:31]),
            (xt_ref, ct_ref, seg_ref, g1_ref, g2_ref, wp_ref, wo_ref, wg_ref, wu_ref, wdt_ref, *gain_state),
        ))
    ]
    for n in (2, 3, 0, 5, 6, 1, 4, 7, 8, 9, 10, 11, 12, 13, 14, 15):
        loads[n].start()
    ex.greet()
    loads[2].wait()

    seg_row = seg_ref[...].astype(F32)
    seg_cols = jnp.broadcast_to(seg_row, (8, rows)).T[:, :1]
    starts = jnp.zeros((1, rows), F32)
    for k in range(0, rows, 128):
        lower = (seg_cols[k : k + 128] < seg_row).astype(F32)
        starts = starts + jnp.sum(lower, axis=0, keepdims=True)
    places_row = lax.broadcasted_iota(jnp.int32, (1, rows), 1).astype(F32)
    index = lax.broadcasted_iota(jnp.int32, (half, 1), 0).astype(F32)
    frequency = jnp.exp(index * (-2.0 * math.log(THETA) / HS))
    angles = frequency * (places_row - starts)
    cosine = jnp.cos(angles)
    sine = jnp.sin(angles)

    loads[3].wait()
    gain1 = column(g1_ref, D)
    loads[5].wait()
    loads[0].wait()
    dgain[...] = jnp.zeros_like(dgain)

    def unit_one(cols):
        xf = xt_ref[:, cols].astype(F32)
        scale = lax.rsqrt(jnp.mean(xf * xf, axis=0, keepdims=True) + EPSILON)
        return xf * scale, scale

    def project(wpt):
        wpt[...] = wp_ref[...].T
        for r in range(tiles):
            r0 = r * T
            cs = cosine[:, r0 : r0 + T]
            sn = sine[:, r0 : r0 + T]
            unit, _ = unit_one(slice(r0, r0 + T))
            normed = (unit * gain1).astype(BF16)
            nt[:, r0 : r0 + T] = normed
            joined = dot(wpt[...], normed)
            for h in range(H + 2 * KV):
                jt = joined[h * HS : (h + 1) * HS]
                a = jt[:half]
                b = jt[half:]
                if h < H:
                    qt[h, 0:half, r0 : r0 + T] = ((a * cs - b * sn) * (HS**-0.5)).astype(BF16)
                    qt[h, half:HS, r0 : r0 + T] = ((b * cs + a * sn) * (HS**-0.5)).astype(BF16)
                elif h < H + KV:
                    kt_[h - H, 0:half, r0 : r0 + T] = (a * cs - b * sn).astype(BF16)
                    kt_[h - H, half:HS, r0 : r0 + T] = (b * cs + a * sn).astype(BF16)
                else:
                    vt[h - H - KV, :, r0 : r0 + T] = jt.astype(BF16)

    pl.run_scoped(project, pltpu.VMEM((QKV, D), BF16))
    for n in range(KV):
        kn[n] = kt_[n].T
        vn[n] = vt[n].T

    def ef(k, i):
        if k < 2:
            return k * T, i * T
        return 2 * T, (i - 2 + 2 * (k - 2)) * T

    def e_store(h):
        slot = h % 2 if isinstance(h, int) else lax.rem(h, 2)
        return pltpu.make_async_copy(es.at[slot], e_hbm.at[h], e_sem.at[slot])

    def e_load(h):
        slot = h % 2
        return pltpu.make_async_copy(e_hbm.at[h], es.at[slot], e_sem.at[slot])

    def forward(bias, sc):
        for i in range(tiles):
            for k in range(i + 1):
                kk = lax.broadcasted_iota(jnp.int32, (T, T), 0).astype(F32) + float(k * T)
                ok = kk >= starts[:, i * T : (i + 1) * T]
                if k == i:
                    qq = lax.broadcasted_iota(jnp.int32, (T, T), 1).astype(F32) + float(i * T)
                    ok = ok & (kk <= qq)
                bias[i * (i + 1) // 2 + k] = jnp.where(ok, 0.0, NEGATIVE)

        def head(h, _):
            n = h // GROUP
            slot = lax.rem(h, 2)

            @pl.when(h >= 2)
            def _():
                e_store(h - 2).wait()

            for i in range(tiles):
                q = qt[h, :, i * T : (i + 1) * T]
                peak = None
                for k in range(i + 1):
                    s = dot(kn[n, k * T : (k + 1) * T, :], q) + bias[i * (i + 1) // 2 + k]
                    sc[i % 2, k] = s
                    top = jnp.max(s, axis=0, keepdims=True)
                    peak = top if peak is None else jnp.maximum(peak, top)
                total_ = jnp.zeros((1, T), F32)
                out = jnp.zeros((HS, T), F32)
                for k in range(i + 1):
                    e = jnp.exp(sc[i % 2, k] - peak)
                    total_ = total_ + jnp.sum(e, axis=0, keepdims=True)
                    e16 = e.astype(BF16)
                    a, b = ef(k, i)
                    es[slot, a : a + T, b : b + T] = e16
                    out = out + dot(vt[n, :, k * T : (k + 1) * T], e16)
                inverse = 1.0 / total_
                invl[h, :, i * T : (i + 1) * T] = inverse
                mt[pl.ds(pl.multiple_of(h * HS, HS), HS), i * T : (i + 1) * T] = (
                    out * inverse
                ).astype(BF16)
            e_store(h).start()
            return 0

        lax.fori_loop(0, H, head, 0)
        e_store(H - 2).wait()
        e_store(H - 1).wait()

    pl.run_scoped(
        forward,
        pltpu.VMEM((tiles * (tiles + 1) // 2, T, T), F32),
        pltpu.VMEM((2, tiles, T, T), F32),
    )
    e_load(0).start()
    ex.met()

    RT = 512
    CT = 256

    def feeding(wot, cn, n2, n2t, hid, gg, gu_, res, scale2):
        for n in (1, 4, 6, 7, 8, 9, 10, 11, 12, 13, 14, 15):
            loads[n].wait()
        gain2 = column(g2_ref, D)
        wot[...] = wo_ref[...].T
        cn[...] = ct_ref[...].T

        def mixing(r, _):
            rs = pl.ds(pl.multiple_of(r * T, T), T)
            residual = xt_ref[:, rs].astype(F32) + dot(wot[...], mt[:, rs])
            scale = lax.rsqrt(jnp.mean(residual * residual, axis=0, keepdims=True) + EPSILON)
            res[:, rs] = residual
            scale2[:, rs] = scale
            n2v = (residual * scale * gain2).astype(BF16)
            n2t[:, rs] = n2v
            n2[rs, :] = n2v.T
            return 0

        lax.fori_loop(0, rows // T, mixing, 0)
        def part_of(ref, u, s0, s1):
            return jnp.concatenate(
                [ref[:, s * (FF // 4) + u * LANES : s * (FF // 4) + (u + 1) * LANES] for s in range(s0, s1)], axis=1
            )

        for u in range(3):

            for half_ in range(2):
                js = slice(half_ * CT, (half_ + 1) * CT)

                def tile(r, _):
                    rs = pl.ds(pl.multiple_of(r * RT, RT), RT)
                    gate = dot(n2[rs, :], part_of(wg_ref, u, 2 * half_, 2 * half_ + 2))
                    up_ = dot(n2[rs, :], part_of(wu_ref, u, 2 * half_, 2 * half_ + 2))
                    gh = dot(cn[rs, :], part_of(wdt_ref, u, 2 * half_, 2 * half_ + 2))
                    sg = 0.5 * jnp.tanh(0.5 * gate) + 0.5
                    sl = gate * sg
                    hid[rs, js] = (sl * up_).astype(BF16)
                    gg[rs, js] = (gh * up_ * (sg + sl * (1.0 - sg))).astype(BF16)
                    gu_[rs, js] = (gh * sl).astype(BF16)
                    return 0

                lax.fori_loop(0, rows // RT, tile, 0)
                if u and TILE_TICKS[half_]:
                    ex.tick()
            for b, (left, right) in enumerate(((n2t, gg), (n2t, gu_), (ct_ref, hid))):
                part = dot(left[...], right[...]).astype(BF16)
                for s in range(4):
                    for p in range(4):
                        a, c = (s, p) if b < 2 else (p, s)
                        grads[u, s // 2, s % 2, p // 2, p % 2, b * PR : (b + 1) * PR, :] = part[
                            a * PR : (a + 1) * PR, c * LANES : (c + 1) * LANES
                        ]
            ex.begin(ex.unit(u, 0, 3))

            def back(r, _):
                rs = pl.ds(pl.multiple_of(r * RT, RT), RT)
                gn2 = dot_t(part_of(wg_ref, u, 0, 4), gg[rs, :]) + dot_t(part_of(wu_ref, u, 0, 4), gu_[rs, :])
                gres[:, rs] = gn2 if u == 0 else gres[:, rs] + gn2
                res[:, rs] += dot_t(part_of(wdt_ref, u, 0, 4), hid[rs, :])
                return 0

            lax.fori_loop(0, rows // RT, back, 0)
            if u < 2:
                ex.tick()

        def ending(r, _):
            rs = pl.ds(pl.multiple_of(r * T, T), T)
            n2t[:, rs] = res[:, rs].astype(BF16)
            scale = scale2[:, rs]
            residual = xt_ref[:, rs].astype(F32) + dot(wot[...], mt[:, rs])
            unit = residual * scale
            gn2 = gres[:, rs]
            dgain[:, 1:2] += jnp.sum(gn2 * unit, axis=1, keepdims=True)
            e = gn2 * gain2
            gr = ct_ref[:, rs].astype(F32) + scale * (
                e - unit * jnp.mean(e * unit, axis=0, keepdims=True)
            )
            gres[:, rs] = gr
            gmt[:, rs] = dot(wo_ref[...], gr.astype(BF16)).astype(BF16)
            return 0

        lax.fori_loop(0, rows // T, ending, 0)
        out = pltpu.make_async_copy(n2t, bot_ref, out_sem.at[0])
        out.start()
        part = dot_t(mt[...], gres[...].astype(BF16)).astype(BF16)
        for s in range(4):
            mine = part[s * PR : (s + 1) * PR]
            for p in range(4):
                grads[3, s // 2, s % 2, p // 2, p % 2, :PR, :] = mine[:, p * LANES : (p + 1) * LANES]
            grads[3, s // 2, s % 2, 1, 1, 2 * PR :, 64:] = mine[:, 512:]
        out.wait()

    pl.run_scoped(
        feeding,
        pltpu.VMEM((D, D), BF16),
        pltpu.VMEM((rows, D), BF16),
        pltpu.VMEM((rows, D), BF16),
        pltpu.VMEM((D, rows), BF16),
        pltpu.VMEM((rows, CH), BF16),
        pltpu.VMEM((rows, CH), BF16),
        pltpu.VMEM((rows, CH), BF16),
        pltpu.VMEM((D, rows), F32),
        pltpu.VMEM((1, rows), F32),
    )
    def backward(ds, gjt, dk, dv, cs_ref, sn_ref, tail, *held):
        ex.held, ex.tail = held, tail
        for copy in ex.load_state():
            copy.start()
        ex.begin(ex.unit(3, 0, 1))
        cs_ref[...] = cosine
        sn_ref[...] = sine

        def unrotate(v, base):
            a = v[:half]
            b = v[half:]
            cs = cs_ref[...]
            sn = sn_ref[...]
            gjt[base : base + half, :] = (a * cs + b * sn).astype(BF16)
            gjt[base + half : base + HS, :] = (b * cs - a * sn).astype(BF16)

        def head(h, n):
            slot = h % 2
            hs = slice(h * HS, (h + 1) * HS)
            if h + 1 < H:
                e_load(h + 1).start()

            do = (gmt[hs, :].astype(F32) * invl[h]).astype(BF16)
            delta = jnp.sum(do.astype(F32) * mt[hs, :].astype(F32), axis=0, keepdims=True)
            e_load(h).wait()
            for k in range(tiles):
                ks = slice(k * T, (k + 1) * T)
                for i in range(k, tiles):
                    cols = slice(i * T, (i + 1) * T)
                    a, b = ef(k, i)
                    dp = dot(vn[n, ks, :], do[:, cols]) - delta[:, cols]
                    ds[ks, cols] = (es[slot, a : a + T, b : b + T].astype(F32) * dp).astype(BF16)
                a, b = ef(k, k)
                dv[ks, :] += dot_t(es[slot, a : a + T, b : b + rows - k * T], do[:, k * T :])
                dk[ks, :] += dot_t(ds[ks, k * T :], qt[h, :, k * T :])
            dq = [
                dot(kt_[n, :, : (i + 1) * T], ds[: (i + 1) * T, i * T : (i + 1) * T])
                for i in range(tiles)
            ]
            unrotate(jnp.concatenate(dq, axis=1) * (HS**-0.5), h * HS)

        for n in range(KV):
            dk[...] = jnp.zeros_like(dk)
            dv[...] = jnp.zeros_like(dv)
            for g in range(GROUP):
                head(n * GROUP + g, n)
                if n + g == 0:
                    ex.have_state()
                if HEAD_TICKS[n * GROUP + g]:
                    ex.tick()
            unrotate(dk[...].T, H * HS + n * HS)
            gjt[(H + KV + n) * HS : (H + KV + n + 1) * HS, :] = dv[...].T.astype(BF16)

        for k in range(2):
            part = dot_t(nt[...], gjt[512 * k : min(512 * k + 512, QKV), :]).astype(BF16)
            for s in range(4):
                mine = part[s * PR : (s + 1) * PR]
                for p in range(4):
                    c = p * LANES
                    w = min(part.shape[1] - c, LANES)
                    grads[3, s // 2, s % 2, p // 2, p % 2, (k + 1) * PR : (k + 2) * PR, :w] = mine[
                        :, c : c + w
                    ]
        ex.begin(ex.unit(3, 1, 2))

        for r in range(tiles):
            rs = slice(r * T, (r + 1) * T)
            gn = dot(wp_ref[...], gjt[:, rs])
            unit, scale = unit_one(rs)
            dgain[:, 0:1] += jnp.sum(gn * unit, axis=1, keepdims=True)
            e = gn * gain1
            tg = gres[:, rs] + scale * (e - unit * jnp.mean(e * unit, axis=0, keepdims=True))
            gmt[:, rs] = tg.astype(BF16)
            if r == 1:
                ex.tick()
        out = pltpu.make_async_copy(gmt, tgt_ref, out_sem.at[1])
        out.start()
        for s in range(4):
            gain_ref[s] = dgain[s * PR : (s + 1) * PR, :].T
        ex.begin(ex.gain())
        ex.finish()
        out.wait()

    pl.run_scoped(
        backward,
        pltpu.VMEM((rows, rows), BF16),
        pltpu.VMEM((QKV, rows), BF16),
        pltpu.VMEM((rows, HS), F32),
        pltpu.VMEM((rows, HS), F32),
        pltpu.VMEM((half, rows), F32),
        pltpu.VMEM((half, rows), F32),
        pltpu.VMEM((3, PR, LANES), F32),
        *[pltpu.VMEM((3,) + a.shape, F32) for a in state[:5]],
    )


TILE_TICKS = (0, 1)
HEAD_TICKS = (1, 0, 1, 0, 1, 0, 1, 0, 1)


def run_step(mesh_shape, xt, ct, seg, g1, g2, wp, wo, wg, wu, wdt, state, gain_state):
    rows = xt.shape[1]
    bits = mesh_shape["rep"].bit_length() - 1
    total = float(rows * mesh_shape["rep"] * mesh_shape["shard"])
    vm = pl.BlockSpec(memory_space=pltpu.VMEM)
    hbm = pl.BlockSpec(memory_space=pl.ANY)
    sd = jax.ShapeDtypeStruct
    npeer = bits + 2
    copies = 5 * 24 + 5 * bits + npeer + 3
    piece = (UNIT, LANES)
    v = pltpu.VMEM
    return pl.pallas_call(
        lambda *refs: step_kernel(bits, total, *refs),
        name="step",
        out_shape=(
            sd((D, rows), BF16),
            sd((D, rows), BF16),
            sd((4, 8, PR), F32),
            sd((4, 8, PR), F32),
            sd((UNITS, 2, 2) + piece, BF16),
            sd((UNITS, 2, 2, 2, 2) + piece, BF16),
            sd((H, 3 * T, rows), BF16),
        ),
        in_specs=[hbm] * 31,
        out_specs=(hbm, hbm, vm, vm, hbm, hbm, hbm),
        scratch_shapes=[
            v((D, rows), BF16),
            v((D, rows), BF16),
            v((1, rows), jnp.int32),
            v((D,), BF16),
            v((D,), BF16),
            v((D, QKV), BF16),
            v((D, D), BF16),
            v((D, FF), BF16),
            v((D, FF), BF16),
            v((D, FF), BF16),
        ]
        + [v((PR,), F32)] * 6
        + [
            v((H, HS, rows), BF16),
            v((KV, HS, rows), BF16),
            v((KV, HS, rows), BF16),
            v((KV, rows, HS), BF16),
            v((KV, rows, HS), BF16),
            v((D, rows), BF16),
            v((D, rows), BF16),
            v((D, rows), BF16),
            v((2, 3 * T, rows), BF16),
            v((H, 1, rows), F32),
            v((D, rows), F32),
            v((D, 8), F32),
            v((4, 8, PR), F32),
            v((UNITS, 2, 2, 2, 2) + piece, BF16),
            v((UNITS, 2, 2, 2) + piece, BF16),
            v((UNITS, 2, 2) + piece, BF16),
            v((UNITS, 2) + piece, BF16),
            v((UNITS,) + piece, BF16),
            v((UNITS, bits - 1) + piece, BF16),
            v((UNITS, bits - 2) + piece, BF16),
            v((UNITS, 3, 2, 2) + piece, BF16),
            v((npeer, 4, 8, PR), F32),
            v((npeer, 4, 8, PR), F32),
            v((4, 8, PR), F32),
        ]
        + [pltpu.SemaphoreType.DMA((n,)) for n in (copies, copies, 15, 15, 16, 2, 2)],
        compiler_params=pltpu.CompilerParams(
            vmem_limit_bytes=VMEM_LIMIT, collective_id=0, has_side_effects=True
        ),
    )(xt, ct, seg.reshape(1, rows), g1, g2, wp, wo, wg, wu, wdt, *state, *gain_state)


VMEM_LIMIT = 63 * 2**20


def update_kernel(total, *refs):
    gf_ref, u_ref, gsum_ref, gup_ref = refs[:4]
    rows_in, state, gain_state = refs[4:6], refs[6:21], refs[21:27]
    outs = refs[27:47]
    gain_outs, rounded, gain_rounded, rows_out = refs[47:55], refs[55:60], refs[60:62], refs[62:64]
    gf, low = refs[64:66]
    held, made, wide, rows_held = refs[66:81], refs[81:101], refs[101:106], refs[106:108]
    load_sem, low_sem, gf_sem, out_sem, wide_sem, row_sem = refs[108:]

    loads = {}
    grads = []
    for t in range(4):
        grads.append(pltpu.make_async_copy(gf_ref.at[t], gf.at[t], gf_sem.at[t]))
        grads[-1].start()
    for numbers in ((0, 1, 2), (3, 4)):
        for number in numbers:
            for k in range(3):
                n = 5 * k + number
                loads[n] = pltpu.make_async_copy(state[n], held[n], load_sem.at[n])
                loads[n].start()
    lows = []
    for t in range(4):
        lows.append(pltpu.make_async_copy(u_ref.at[t], low.at[t], low_sem.at[t]))
        lows[-1].start()
    row_loads = []
    for n in range(2):
        row_loads.append(pltpu.make_async_copy(rows_in[n], rows_held[n], row_sem.at[n]))
        row_loads[-1].start()
    stores = []

    def store(src, dst, sem):
        stores.append(pltpu.make_async_copy(src, dst, sem))
        stores[-1].start()

    shard = lax.axis_index("shard")
    x = shard // 2
    for k in range(2):
        whole = jnp.concatenate([gup_ref[s, k : k + 1, :] for s in range(4)], axis=1)
        gain_rounded[k][...] = whole.astype(BF16).reshape(D)
    grad = gsum_ref[shard] / total
    for k in range(2):
        m, v, w = (gain_state[2 * q + k][...].reshape(1, PR) for q in range(3))
        one = grad[k : k + 1]
        velocity, spread, updated = adam(one, m, v, w, BASE_RATE, False)
        for q, value in enumerate((one, updated, velocity, spread)):
            gain_outs[2 * q + k][...] = value.reshape(PR)
    for t in range(4):
        numbers = ((), (), (0, 1, 2), (3, 4))[t]
        grads[t].wait()
        for number in ((0, 1, 2), (), (), (3, 4))[t]:
            for k in range(3):
                loads[5 * k + number].wait()
        for p in range(4):
            for r, lane, nl, number, r0, c0 in blocks(t, p):
                where = (slice(r0, r0 + PR), slice(c0, c0 + nl))
                m, v, w = (held[5 * k + number][where] for k in range(3))
                grad = gf[t, p // 2, p % 2, r : r + PR, lane : lane + nl].astype(F32) / total
                velocity, spread, updated = adam(grad, m, v, w, RATES[number], True)
                for q, value in enumerate((grad, updated, velocity, spread)):
                    made[5 * q + number][where] = value
        for number in numbers:
            for q in range(4):
                n = 5 * q + number
                store(made[n], outs[n], out_sem.at[n])
        lows[t].wait()
        for s in range(4):
            for p in range(4):
                for r, lane, nl, number, r0, c0 in blocks(t, p):
                    if number == 2:
                        c0 += s * (FF // 4)
                    else:
                        r0 = s * PR
                    wide[number][r0 : r0 + PR, c0 : c0 + nl] = low[
                        t, s % 2, x if s < 2 else 1 - x, p // 2, p % 2, r : r + PR, lane : lane + nl
                    ]
        for number in numbers:
            store(wide[number], rounded[number], wide_sem.at[number])
    for n in range(2):
        row_loads[n].wait()
        store(rows_held[n], rows_out[n], row_sem.at[2 + n])
    for copy in stores:
        copy.wait()


def run_update(total, bot, tgt, gf, u, gsum, gup, state, gain_state):
    vm = pl.BlockSpec(memory_space=pltpu.VMEM)
    hbm = pl.BlockSpec(memory_space=pl.ANY)
    sd = jax.ShapeDtypeStruct
    shapes = [a.shape for a in state[:5]]
    full = [(D, FF)] * 3 + [(D, QKV), (D, D)]
    return pl.pallas_call(
        lambda *refs: update_kernel(total, *refs),
        name="update",
        out_shape=tuple(sd(s, F32) for s in shapes * 4)
        + (sd((PR,), F32),) * 8
        + tuple(sd(s, BF16) for s in full)
        + (sd((D,), BF16),) * 2
        + (sd(bot.shape, BF16),) * 2,
        in_specs=[hbm, hbm, vm, vm] + [hbm] * 17 + [vm] * 6,
        out_specs=(hbm,) * 20 + (vm,) * 8 + (hbm,) * 5 + (vm,) * 2 + (hbm,) * 2,
        scratch_shapes=[
            pltpu.VMEM((UNITS, 2, 2, UNIT, LANES), BF16),
            pltpu.VMEM((UNITS, 2, 2, 2, 2, UNIT, LANES), BF16),
        ]
        + [pltpu.VMEM(s, F32) for s in shapes * 3]
        + [pltpu.VMEM(s, F32) for s in shapes * 4]
        + [pltpu.VMEM(s, BF16) for s in full]
        + [pltpu.VMEM(bot.shape, BF16)] * 2
        + [pltpu.SemaphoreType.DMA((n,)) for n in (15, 4, 4, 20, 5, 4)],
        compiler_params=pltpu.CompilerParams(vmem_limit_bytes=62 * 2**20),
    )(gf, u, gsum, gup, bot, tgt, *state, *gain_state)


def solution(mesh):
    mesh_shape = dict(mesh.shape)

    def body(
        tokens, cotangent, segment_ids, current_attention, current_project, current_output,
        current_feeding, current_gating, current_upward, current_downward, *state_all,
    ):
        rows = tokens.shape[0]
        total = float(rows * mesh_shape["rep"] * mesh_shape["shard"])
        state, gain_state = [], []
        for k in range(3):
            at, pr, ou, fe, ga, uw, dw = state_all[7 * k : 7 * k + 7]
            state += [ga, uw, dw.T, pr, ou]
            gain_state += [at, fe]
        bot, tgt, gsum, gup, gf, u, _ = run_step(
            mesh_shape, tokens.T, cotangent.T, segment_ids, current_attention, current_feeding, current_project,
            current_output, current_gating, current_upward, current_downward.T, state, gain_state,
        )
        out = run_update(total, bot, tgt, gf, u, gsum, gup, state, gain_state)
        results = [out[35].T, out[36].T]
        for q in range(4):
            ga, uw, dw, pr, ou = out[5 * q : 5 * q + 5]
            at, fe = out[20 + 2 * q : 22 + 2 * q]
            results += [at, pr, ou, fe, ga, uw, dw.T]
        ga, uw, dw, pr, ou = out[28:33]
        at, fe = out[33:35]
        return (*results, at, pr, ou, fe, ga, uw, dw.T)

    row, vec = P("shard", None), P("shard")
    seven = (vec, row, row, vec, row, row, row)
    spread = P(("shard", "rep"), None)
    in_specs = (spread, spread, P(("shard", "rep"))) + (P(),) * 7 + seven * 3
    out_specs = (spread, spread) + seven * 4 + (P(),) * 7
    return jax.shard_map(body, mesh=mesh, in_specs=in_specs, out_specs=out_specs, check_vma=False)
```

```python
import math

import jax
import jax.numpy as jnp
from jax import lax
from jax.experimental import pallas as pl
from jax.experimental.pallas import tpu as pltpu
from jax.sharding import PartitionSpec as P

D = 576
H = 9
KV = 3
HS = 64
FF = 1536
QKV = 960
STEP = 5
GROUP = H // KV

EPSILON = 1e-05
THETA = 10000.0
BETA = 0.5
ADAM_EPSILON = 1e-08
DECAY = 0.1
NEGATIVE = -1e30
BASE_RATE = 0.3

F32 = jnp.float32
BF16 = jnp.bfloat16
T = 256
PR = D // 4
LANES = 128
UNIT = 3 * PR
CH = 512
UNITS = 4


def dot(a, b):
    return jnp.dot(a, b, preferred_element_type=F32)


def dot_t(a, b):
    return lax.dot_general(a, b, (((1,), (1,)), ((), ())), preferred_element_type=F32)

MESH = pl.DeviceIdType.MESH
RATES = tuple(
    BASE_RATE * v
    for v in (float(D) ** -0.5, float(D) ** -0.5, float(FF) ** -0.5, float(D) ** -0.5, float(max(D // 96, 1)) ** -0.5)
)
CORRECTION = 1.0 - BETA**STEP


def blocks(u, p):
    if u < 3:
        c = p * (FF // 4) + u * LANES
        return [(0, 0, LANES, 0, 0, c), (PR, 0, LANES, 1, 0, c), (2 * PR, 0, LANES, 2, p * PR, u * LANES)]
    out = [(0, 0, LANES, 4, 0, p * LANES), (PR, 0, LANES, 3, 0, p * LANES)]
    if p < 3:
        return out + [(2 * PR, 0, LANES, 3, 0, 512 + p * LANES)]
    return out + [(2 * PR, 0, 64, 3, 0, 896), (2 * PR, 64, 64, 4, 0, 512)]


def adam(grad, master, moment, variance, rate, decay):
    velocity = BETA * moment + (1.0 - BETA) * grad
    spread = BETA * variance + (1.0 - BETA) * grad * grad
    direction = velocity / CORRECTION / (jnp.sqrt(spread / CORRECTION) + ADAM_EPSILON)
    if decay:
        direction = direction + DECAY * master
    return velocity, spread, master - rate * direction


def add_into(dst, a, b):
    dst[...] = (a[...].astype(F32) + b[...].astype(F32)).astype(BF16)


def column(ref, size):
    row = jnp.broadcast_to(ref[...].astype(F32).reshape(1, size), (8, size))
    return row.T[:, :1]


class Exchange:
    def __init__(self, bits, total, refs):
        self.__dict__.update(refs)
        self.bits, self.total = bits, total
        self.shard, self.rep = lax.axis_index("shard"), lax.axis_index("rep")
        self.x, self.core = self.shard // 2, lax.rem(self.shard, 2)
        self.y, self.zl = lax.rem(self.rep, 2), lax.rem(self.rep // 2, 2)
        self.peer_c = (self.flip(self.shard, 0), self.rep)
        self.peer_x = (self.flip(self.shard, 1), self.rep)
        self.peer_r = [(self.shard, self.flip(self.rep, b)) for b in range(bits)]
        self.peers = [self.peer_c, self.peer_x] + self.peer_r
        self.other = self.flip(self.shard, 1)
        self.not_x, self.not_core, self.not_y, self.not_zl = (1 - v for v in (self.x, self.core, self.y, self.zl))
        self.sent, self.kept, self.live = [], [], []

    @staticmethod
    def flip(index, bit):
        size = 1 << bit
        return index + size - 2 * size * lax.rem(index // size, 2)

    def greet(self):
        self.barrier = pltpu.get_barrier_semaphore()
        for peer in self.peers:
            pl.semaphore_signal(self.barrier, inc=1, device_id=peer, device_id_type=MESH)

    def met(self):
        pl.semaphore_wait(self.barrier, len(self.peers))

    def send(self, src, dst, peer):
        n = len(self.sent)

        def make():
            return pltpu.make_async_remote_copy(
                src_ref=src(), dst_ref=dst(), send_sem=self.send_sem.at[n], recv_sem=self.recv_sem.at[n],
                device_id=peer, device_id_type=MESH,
            )

        make().start()
        self.sent.append(make)
        return make

    def keep(self, src, dst):
        n = len(self.kept)

        def make():
            return pltpu.make_async_copy(src(), dst(), self.keep_sem.at[n])

        make().start()
        self.kept.append(make)

    def begin(self, flow, group=None):
        next(flow)
        self.live.append((flow, group))

    def tick(self, *groups):
        for entry in sorted(self.live, key=lambda e: e[1] is not None):
            if entry[1] is None or entry[1] in groups:
                try:
                    next(entry[0])
                except StopIteration:
                    self.live.remove(entry)

    def finish(self):
        turn = 1
        while self.live:
            self.tick(turn)
            turn = 1 - turn
        for copy in self.sent:
            copy().wait_send()
        for copy in self.kept:
            copy().wait()

    def load_state(self):
        for number, held in enumerate(self.held):
            for k in range(3):
                n = 5 * k + number
                yield pltpu.make_async_copy(self.state[n], held.at[k], self.st_sem.at[n])

    def have_state(self):
        for copy in self.load_state():
            copy.wait()
        for k in range(3):
            self.tail[k] = jnp.concatenate([self.held[3][k, :, 896:], self.held[4][k, :, 512:]], axis=1)

    def gain(self):
        gains, gs, gr, gu = self.gain_ref, self.gs, self.grc, self.gu
        copy = self.send(lambda: gains, lambda: gr.at[0], self.peers[0])
        yield
        last = len(self.peers) - 1
        for b in range(last + 1):
            copy().wait_recv()
            gs[b] = (gains[...] if b == 0 else gs[b - 1]) + gr[b]
            if b < last:
                copy = self.send(lambda b=b: gs.at[b], lambda b=b: gr.at[b + 1], self.peers[b + 1])
                yield
        self.gsum_ref[...] = gs[last]
        shard, other = self.shard, self.other
        grad = gs[last, shard] / self.total
        for k in range(2):
            m, v, w = (self.gain_state[2 * q + k][...].reshape(1, PR) for q in range(3))
            gu[shard, k : k + 1, :] = adam(grad[k : k + 1], m, v, w, BASE_RATE, False)[2]
        copy = self.send(lambda: gu.at[shard], lambda: gu.at[shard], self.peer_x)
        one = self.send(lambda: gu.at[shard], lambda: gu.at[shard], self.peer_c)
        yield
        copy().wait_recv()
        two = self.send(lambda: gu.at[other], lambda: gu.at[other], self.peer_c)
        yield
        one().wait_recv()
        two().wait_recv()
        self.gup_ref[...] = gu[...]

    def update(self, u, b, pieces):
        rs = slice(b * PR, (b + 1) * PR)

        def lanes(c):
            return pl.ds(c if isinstance(c, int) else pl.multiple_of(c, LANES), LANES)

        for py, pz in pieces:
            p = 2 * py + pz
            number = b if u < 3 else (4, 3, 3)[b]
            held, rate = self.held[number], RATES[number]
            if u < 3 and b == 2:
                r0 = p * PR if isinstance(p, int) else pl.multiple_of(p * PR, PR)
                state = [held[k, pl.ds(r0, PR), u * LANES : (u + 1) * LANES] for k in range(3)]
            elif u < 3:
                state = [held[k, :, lanes(p * (FF // 4) + u * LANES)] for k in range(3)]
            elif b < 2:
                state = [held[k, :, lanes(p * LANES)] for k in range(3)]
            else:
                if isinstance(p, int):
                    state = [self.tail[k] if p == 3 else held[k, :, lanes(512 + p * LANES)] for k in range(3)]
                else:
                    near = lanes(512 + jnp.minimum(p, 2) * LANES)
                    state = [jnp.where(p == 3, self.tail[k], held[k, :, near]) for k in range(3)]
                lane = lax.broadcasted_iota(jnp.int32, (PR, LANES), 1) + LANES * p
                rate = jnp.where(lane < QKV - 512, RATES[3], RATES[4])
            grad = self.agb[u, 2, py, pz, rs].astype(F32) / self.total
            self.agb[u, 0, py, pz, rs] = adam(grad, *state, rate, True)[2].astype(BF16)

    def unit(self, u, first, count):
        own = {"x": self.x, "y": self.y, "z": self.zl}
        far = {"x": self.not_x, "y": self.not_y, "z": self.not_zl}
        peer = {"x": self.peer_x, "y": self.peer_r[0], "z": self.peer_r[1]}
        core, not_core = self.core, self.not_core
        g, r1, s4, r5, agb = self.grads, self.r1, self.s4, self.r5, self.agb
        span = range(first, first + count)
        rs = pl.ds(first * PR, count * PR)

        def rows(b):
            return pl.ds(b * PR, PR)

        copy = self.send(lambda: g.at[u, :, not_core, :, :, rs], lambda: r1.at[u, :, :, :, rs], self.peer_c)
        yield
        copy().wait_recv()

        def both(n, _):
            i, p, q = n // 4, lax.rem(n // 2, 2), lax.rem(n, 2)
            add_into(g.at[u, i, core, p, q, rs], g.at[u, i, core, p, q, rs], r1.at[u, i, p, q, rs])
            return 0

        lax.fori_loop(0, 8, both, 0)

        def at(index):
            return (u, index["x"], core, index["y"], index["z"])

        for stage in range(3):
            landed = (self.r2, self.r3, self.r4)[stage]
            copies = []
            for b in span:
                order = HALVES[b]
                index = {d: own[d] for d in order[:stage]}
                index.update({d: slice(None) for d in order[stage + 1 :]})
                index[order[stage]] = far[order[stage]]
                free = (slice(None),) * (2 - stage)
                copies.append(self.send(
                    lambda w=at(index), b=b: g.at[w + (rows(b),)],
                    lambda f=free, b=b, landed=landed: landed.at[(u,) + f + (rows(b),)],
                    peer[order[stage]],
                ))
            yield
            for copy in copies:
                copy().wait_recv()
            for b in span:
                order = HALVES[b]
                later = sorted(order[stage + 1 :])
                for n in range(1 << len(later)):
                    index = {d: own[d] for d in order[: stage + 1]}
                    bits = tuple(n >> k & 1 for k in reversed(range(len(later))))
                    index.update(zip(later, bits))
                    w = at(index) + (rows(b),)
                    if stage < 2:
                        add_into(g.at[w], g.at[w], landed.at[(u,) + bits + (rows(b),)])
                    else:
                        add_into(s4.at[u, 0, rows(b)], g.at[w], landed.at[u, rows(b)])

        last = self.bits - 2
        for k in range(last):
            copy = self.send(lambda k=k: s4.at[u, k, rs], lambda k=k: r5.at[u, k, rs], self.peer_r[2 + k])
            yield
            copy().wait_recv()
            add_into(s4.at[u, k + 1, rs], s4.at[u, k, rs], r5.at[u, k, rs])
        y, zl = self.y, self.zl
        agb[u, 2, y, zl, rs] = s4[u, last, rs]

        for stage in range(3):
            copies = []
            for b in span:
                order = GATHERS[b]
                d = order[stage]
                known = order[:stage]
                index = (slice(None) if "y" in known else y, slice(None) if "z" in known else zl, rows(b))
                if d == "x":
                    ys = range(2) if "y" in known else (y,)
                    zs = range(2) if "z" in known else (zl,)
                    self.update(u, b, [(i, j) for i in ys for j in zs])
                    copies.append(self.send(
                        lambda w=index: agb.at[(u, 0) + w], lambda w=index: agb.at[(u, 1) + w], peer[d]
                    ))
                    continue
                kinds = pl.ds(1, 2) if "x" in known else 2
                copies.append(self.send(
                    lambda w=index, k=kinds: agb.at[(u, k) + w], lambda w=index, k=kinds: agb.at[(u, k) + w], peer[d]
                ))
            yield
            for copy in copies:
                copy().wait_recv()
        self.keep(lambda: agb.at[u, 2, :, :, rs], lambda: self.gf_ref.at[u, :, :, rs])
        for b in span:
            known = GATHERS[b][: GATHERS[b].index("x")]
            if known == "":
                self.update(u, b, [(self.not_y, zl), (y, self.not_zl), (self.not_y, self.not_zl)])
            elif known == "y":
                self.update(u, b, [(i, self.not_zl) for i in range(2)])
            elif known == "z":
                self.update(u, b, [(self.not_y, i) for i in range(2)])
        self.keep(lambda: agb.at[u, pl.ds(0, 2), :, :, rs], lambda: self.u_ref.at[u, core, :, :, :, rs])
        copy = self.send(
            lambda: agb.at[u, pl.ds(0, 2), :, :, rs], lambda: self.u_ref.at[u, core, :, :, :, rs], self.peer_c
        )
        yield
        copy().wait_recv()


HALVES = ("xyz", "yzx", "zxy")
GATHERS = ("zyx", "xzy", "yxz")


def step_kernel(bits, total, *refs):
    ins, state = refs[:10], refs[10:25]
    bot_ref, tgt_ref, gsum_ref, gup_ref, gf_ref, u_ref, e_hbm = refs[31:38]
    (
        xt_ref, ct_ref, seg_ref, g1_ref, g2_ref, wp_ref, wo_ref, wg_ref, wu_ref, wdt_ref, *gain_state,
        qt, kt_, vt, kn, vn, nt, mt, gmt, es, invl, gres, dgain, gain_ref,
        grads, r1, r2, r3, r4, s4, r5, agb, gs, grc, gu,
        send_sem, recv_sem, keep_sem, st_sem, in_sem, e_sem, out_sem,
    ) = refs[38:]
    rows = xt_ref.shape[1]
    tiles = rows // T
    half = HS // 2
    ex = Exchange(bits, total, dict(
        state=state, gain_state=gain_state, gsum_ref=gsum_ref, gup_ref=gup_ref, gf_ref=gf_ref, u_ref=u_ref,
        gain_ref=gain_ref, grads=grads, r1=r1, r2=r2, r3=r3, r4=r4, s4=s4, r5=r5, agb=agb, gs=gs, grc=grc, gu=gu,
        send_sem=send_sem, recv_sem=recv_sem, keep_sem=keep_sem, st_sem=st_sem,
    ))

    loads = [
        pltpu.make_async_copy(src, dst, in_sem.at[n])
        for n, (src, dst) in enumerate(zip(
            tuple(ins) + tuple(refs[25:31]),
            (xt_ref, ct_ref, seg_ref, g1_ref, g2_ref, wp_ref, wo_ref, wg_ref, wu_ref, wdt_ref, *gain_state),
        ))
    ]
    for n in (2, 3, 0, 5, 6, 1, 4, 7, 8, 9, 10, 11, 12, 13, 14, 15):
        loads[n].start()
    ex.greet()
    loads[2].wait()

    seg_row = seg_ref[...].astype(F32)
    seg_cols = jnp.broadcast_to(seg_row, (8, rows)).T[:, :1]
    starts = jnp.zeros((1, rows), F32)
    for k in range(0, rows, 128):
        lower = (seg_cols[k : k + 128] < seg_row).astype(F32)
        starts = starts + jnp.sum(lower, axis=0, keepdims=True)
    places_row = lax.broadcasted_iota(jnp.int32, (1, rows), 1).astype(F32)
    index = lax.broadcasted_iota(jnp.int32, (half, 1), 0).astype(F32)
    frequency = jnp.exp(index * (-2.0 * math.log(THETA) / HS))
    angles = frequency * (places_row - starts)
    cosine = jnp.cos(angles)
    sine = jnp.sin(angles)

    loads[3].wait()
    gain1 = column(g1_ref, D)
    loads[5].wait()
    loads[0].wait()
    dgain[...] = jnp.zeros_like(dgain)

    def unit_one(cols):
        xf = xt_ref[:, cols].astype(F32)
        scale = lax.rsqrt(jnp.mean(xf * xf, axis=0, keepdims=True) + EPSILON)
        return xf * scale, scale

    def project(wpt):
        wpt[...] = wp_ref[...].T
        for r in range(tiles):
            r0 = r * T
            cs = cosine[:, r0 : r0 + T]
            sn = sine[:, r0 : r0 + T]
            unit, _ = unit_one(slice(r0, r0 + T))
            normed = (unit * gain1).astype(BF16)
            nt[:, r0 : r0 + T] = normed
            joined = dot(wpt[...], normed)
            for h in range(H + 2 * KV):
                jt = joined[h * HS : (h + 1) * HS]
                a = jt[:half]
                b = jt[half:]
                if h < H:
                    qt[h, 0:half, r0 : r0 + T] = ((a * cs - b * sn) * (HS**-0.5)).astype(BF16)
                    qt[h, half:HS, r0 : r0 + T] = ((b * cs + a * sn) * (HS**-0.5)).astype(BF16)
                elif h < H + KV:
                    kt_[h - H, 0:half, r0 : r0 + T] = (a * cs - b * sn).astype(BF16)
                    kt_[h - H, half:HS, r0 : r0 + T] = (b * cs + a * sn).astype(BF16)
                else:
                    vt[h - H - KV, :, r0 : r0 + T] = jt.astype(BF16)

    pl.run_scoped(project, pltpu.VMEM((QKV, D), BF16))
    for n in range(KV):
        kn[n] = kt_[n].T
        vn[n] = vt[n].T

    def ef(k, i):
        if k < 2:
            return k * T, i * T
        return 2 * T, (i - 2 + 2 * (k - 2)) * T

    def e_copies(h, out):
        slot = h % 2 if isinstance(h, int) else lax.rem(h, 2)
        for n in range(3):
            here, there = es.at[slot, pl.ds(n * T, T)], e_hbm.at[h, pl.ds(n * T, T)]
            pair = (here, there) if out else (there, here)
            yield pltpu.make_async_copy(*pair, e_sem.at[slot, n])

    def e_start(h, out):
        for copy in e_copies(h, out):
            copy.start()

    def e_wait(h, out):
        for copy in e_copies(h, out):
            copy.wait()

    def forward(bias, sc):
        for i in range(tiles):
            for k in range(i + 1):
                kk = lax.broadcasted_iota(jnp.int32, (T, T), 0).astype(F32) + float(k * T)
                ok = kk >= starts[:, i * T : (i + 1) * T]
                if k == i:
                    qq = lax.broadcasted_iota(jnp.int32, (T, T), 1).astype(F32) + float(i * T)
                    ok = ok & (kk <= qq)
                bias[i * (i + 1) // 2 + k] = jnp.where(ok, 0.0, NEGATIVE)

        def head(h, _):
            n = h // GROUP
            slot = lax.rem(h, 2)

            @pl.when(h >= 2)
            def _():
                e_wait(h - 2, True)

            for i in range(tiles):
                q = qt[h, :, i * T : (i + 1) * T]
                peak = None
                for k in range(i + 1):
                    s = dot(kn[n, k * T : (k + 1) * T, :], q) + bias[i * (i + 1) // 2 + k]
                    sc[i % 2, k] = s
                    top = jnp.max(s, axis=0, keepdims=True)
                    peak = top if peak is None else jnp.maximum(peak, top)
                total_ = jnp.zeros((1, T), F32)
                out = jnp.zeros((HS, T), F32)
                for k in range(i + 1):
                    e = jnp.exp(sc[i % 2, k] - peak)
                    total_ = total_ + jnp.sum(e, axis=0, keepdims=True)
                    e16 = e.astype(BF16)
                    a, b = ef(k, i)
                    es[slot, a : a + T, b : b + T] = e16
                    out = out + dot(vt[n, :, k * T : (k + 1) * T], e16)
                inverse = 1.0 / total_
                invl[h, :, i * T : (i + 1) * T] = inverse
                mt[pl.ds(pl.multiple_of(h * HS, HS), HS), i * T : (i + 1) * T] = (
                    out * inverse
                ).astype(BF16)
            e_start(h, True)
            return 0

        lax.fori_loop(0, H, head, 0)
        e_wait(H - 2, True)
        e_wait(H - 1, True)

    pl.run_scoped(
        forward,
        pltpu.VMEM((tiles * (tiles + 1) // 2, T, T), F32),
        pltpu.VMEM((2, tiles, T, T), F32),
    )
    e_start(0, False)
    ex.met()

    RT = 512
    CT = 256

    def feeding(wot, cn, n2, n2t, hid, gg, gu_, res, scale2):
        for n in (1, 4, 6, 7, 8, 9, 10, 11, 12, 13, 14, 15):
            loads[n].wait()
        gain2 = column(g2_ref, D)
        wot[...] = wo_ref[...].T
        cn[...] = ct_ref[...].T

        def mixing(r, _):
            rs = pl.ds(pl.multiple_of(r * T, T), T)
            residual = xt_ref[:, rs].astype(F32) + dot(wot[...], mt[:, rs])
            scale = lax.rsqrt(jnp.mean(residual * residual, axis=0, keepdims=True) + EPSILON)
            res[:, rs] = residual
            scale2[:, rs] = scale
            n2v = (residual * scale * gain2).astype(BF16)
            n2t[:, rs] = n2v
            n2[rs, :] = n2v.T
            return 0

        lax.fori_loop(0, rows // T, mixing, 0)
        def part_of(ref, u, s0, s1):
            return jnp.concatenate(
                [ref[:, s * (FF // 4) + u * LANES : s * (FF // 4) + (u + 1) * LANES] for s in range(s0, s1)], axis=1
            )

        for u in range(3):

            for half_ in range(2):
                js = slice(half_ * CT, (half_ + 1) * CT)

                def tile(r, _):
                    rs = pl.ds(pl.multiple_of(r * RT, RT), RT)
                    gate = dot(n2[rs, :], part_of(wg_ref, u, 2 * half_, 2 * half_ + 2))
                    up_ = dot(n2[rs, :], part_of(wu_ref, u, 2 * half_, 2 * half_ + 2))
                    gh = dot(cn[rs, :], part_of(wdt_ref, u, 2 * half_, 2 * half_ + 2))
                    sg = 0.5 * jnp.tanh(0.5 * gate) + 0.5
                    sl = gate * sg
                    hid[rs, js] = (sl * up_).astype(BF16)
                    gg[rs, js] = (gh * up_ * (sg + sl * (1.0 - sg))).astype(BF16)
                    gu_[rs, js] = (gh * sl).astype(BF16)
                    return 0

                lax.fori_loop(0, rows // RT, tile, 0)
                if u and half_:
                    ex.tick(0, 1)
            for b, (left, right) in enumerate(((n2t, gg), (n2t, gu_), (ct_ref, hid))):
                part = dot(left[...], right[...]).astype(BF16)
                for s in range(4):
                    for p in range(4):
                        a, c = (s, p) if b < 2 else (p, s)
                        grads[u, s // 2, s % 2, p // 2, p % 2, b * PR : (b + 1) * PR, :] = part[
                            a * PR : (a + 1) * PR, c * LANES : (c + 1) * LANES
                        ]
            ex.begin(ex.unit(u, 0, 3), u % 2)

            def back(r, _):
                rs = pl.ds(pl.multiple_of(r * RT, RT), RT)
                gn2 = dot_t(part_of(wg_ref, u, 0, 4), gg[rs, :]) + dot_t(part_of(wu_ref, u, 0, 4), gu_[rs, :])
                gres[:, rs] = gn2 if u == 0 else gres[:, rs] + gn2
                res[:, rs] += dot_t(part_of(wdt_ref, u, 0, 4), hid[rs, :])
                return 0

            lax.fori_loop(0, rows // RT, back, 0)
            if u < 2:
                ex.tick(0, 1)

        def ending(r, _):
            rs = pl.ds(pl.multiple_of(r * T, T), T)
            n2t[:, rs] = res[:, rs].astype(BF16)
            scale = scale2[:, rs]
            residual = xt_ref[:, rs].astype(F32) + dot(wot[...], mt[:, rs])
            unit = residual * scale
            gn2 = gres[:, rs]
            dgain[:, 1:2] += jnp.sum(gn2 * unit, axis=1, keepdims=True)
            e = gn2 * gain2
            gr = ct_ref[:, rs].astype(F32) + scale * (
                e - unit * jnp.mean(e * unit, axis=0, keepdims=True)
            )
            gres[:, rs] = gr
            gmt[:, rs] = dot(wo_ref[...], gr.astype(BF16)).astype(BF16)
            return 0

        lax.fori_loop(0, rows // T, ending, 0)
        out = pltpu.make_async_copy(n2t, bot_ref, out_sem.at[0])
        out.start()
        part = dot_t(mt[...], gres[...].astype(BF16)).astype(BF16)
        for s in range(4):
            mine = part[s * PR : (s + 1) * PR]
            for p in range(4):
                grads[3, s // 2, s % 2, p // 2, p % 2, :PR, :] = mine[:, p * LANES : (p + 1) * LANES]
            grads[3, s // 2, s % 2, 1, 1, 2 * PR :, 64:] = mine[:, 512:]
        out.wait()

    pl.run_scoped(
        feeding,
        pltpu.VMEM((D, D), BF16),
        pltpu.VMEM((rows, D), BF16),
        pltpu.VMEM((rows, D), BF16),
        pltpu.VMEM((D, rows), BF16),
        pltpu.VMEM((rows, CH), BF16),
        pltpu.VMEM((rows, CH), BF16),
        pltpu.VMEM((rows, CH), BF16),
        pltpu.VMEM((D, rows), F32),
        pltpu.VMEM((1, rows), F32),
    )
    def backward(ds, gjt, dk, dv, cs_ref, sn_ref, tail, *held):
        ex.held, ex.tail = held, tail
        for copy in ex.load_state():
            copy.start()
        ex.begin(ex.unit(3, 0, 1), 1)
        cs_ref[...] = cosine
        sn_ref[...] = sine

        def unrotate(v, base):
            a = v[:half]
            b = v[half:]
            cs = cs_ref[...]
            sn = sn_ref[...]
            gjt[base : base + half, :] = (a * cs + b * sn).astype(BF16)
            gjt[base + half : base + HS, :] = (b * cs - a * sn).astype(BF16)

        def head(h, n):
            slot = h % 2
            hs = slice(h * HS, (h + 1) * HS)
            if h + 1 < H:
                e_start(h + 1, False)

            do = (gmt[hs, :].astype(F32) * invl[h]).astype(BF16)
            delta = jnp.sum(do.astype(F32) * mt[hs, :].astype(F32), axis=0, keepdims=True)
            e_wait(h, False)
            for k in range(tiles):
                ks = slice(k * T, (k + 1) * T)
                for i in range(k, tiles):
                    cols = slice(i * T, (i + 1) * T)
                    a, b = ef(k, i)
                    dp = dot(vn[n, ks, :], do[:, cols]) - delta[:, cols]
                    ds[ks, cols] = (es[slot, a : a + T, b : b + T].astype(F32) * dp).astype(BF16)
                a, b = ef(k, k)
                dv[ks, :] += dot_t(es[slot, a : a + T, b : b + rows - k * T], do[:, k * T :])
                dk[ks, :] += dot_t(ds[ks, k * T :], qt[h, :, k * T :])
            dq = [
                dot(kt_[n, :, : (i + 1) * T], ds[: (i + 1) * T, i * T : (i + 1) * T])
                for i in range(tiles)
            ]
            unrotate(jnp.concatenate(dq, axis=1) * (HS**-0.5), h * HS)

        for n in range(KV):
            dk[...] = jnp.zeros_like(dk)
            dv[...] = jnp.zeros_like(dv)
            for g in range(GROUP):
                head(n * GROUP + g, n)
                if n * GROUP + g == 1:
                    ex.have_state()
                ex.tick((n * GROUP + g + 1) % 2)
            unrotate(dk[...].T, H * HS + n * HS)
            gjt[(H + KV + n) * HS : (H + KV + n + 1) * HS, :] = dv[...].T.astype(BF16)

        for k in range(2):
            part = dot_t(nt[...], gjt[512 * k : min(512 * k + 512, QKV), :]).astype(BF16)
            for s in range(4):
                mine = part[s * PR : (s + 1) * PR]
                for p in range(4):
                    c = p * LANES
                    w = min(part.shape[1] - c, LANES)
                    grads[3, s // 2, s % 2, p // 2, p % 2, (k + 1) * PR : (k + 2) * PR, :w] = mine[
                        :, c : c + w
                    ]
        ex.begin(ex.unit(3, 1, 2))

        for r in range(tiles):
            rs = slice(r * T, (r + 1) * T)
            gn = dot(wp_ref[...], gjt[:, rs])
            unit, scale = unit_one(rs)
            dgain[:, 0:1] += jnp.sum(gn * unit, axis=1, keepdims=True)
            e = gn * gain1
            tg = gres[:, rs] + scale * (e - unit * jnp.mean(e * unit, axis=0, keepdims=True))
            gmt[:, rs] = tg.astype(BF16)
            if r == 1:
                ex.tick(0)
        out = pltpu.make_async_copy(gmt, tgt_ref, out_sem.at[1])
        out.start()
        for s in range(4):
            gain_ref[s] = dgain[s * PR : (s + 1) * PR, :].T
        ex.begin(ex.gain())
        ex.finish()
        out.wait()

    pl.run_scoped(
        backward,
        pltpu.VMEM((rows, rows), BF16),
        pltpu.VMEM((QKV, rows), BF16),
        pltpu.VMEM((rows, HS), F32),
        pltpu.VMEM((rows, HS), F32),
        pltpu.VMEM((half, rows), F32),
        pltpu.VMEM((half, rows), F32),
        pltpu.VMEM((3, PR, LANES), F32),
        *[pltpu.VMEM((3,) + a.shape, F32) for a in state[:5]],
    )


def run_step(mesh_shape, xt, ct, seg, g1, g2, wp, wo, wg, wu, wdt, state, gain_state):
    rows = xt.shape[1]
    bits = mesh_shape["rep"].bit_length() - 1
    total = float(rows * mesh_shape["rep"] * mesh_shape["shard"])
    vm = pl.BlockSpec(memory_space=pltpu.VMEM)
    hbm = pl.BlockSpec(memory_space=pl.ANY)
    sd = jax.ShapeDtypeStruct
    npeer = bits + 2
    copies = 5 * 24 + 5 * bits + npeer + 3
    piece = (UNIT, LANES)
    v = pltpu.VMEM
    return pl.pallas_call(
        lambda *refs: step_kernel(bits, total, *refs),
        name="step",
        out_shape=(
            sd((D, rows), BF16),
            sd((D, rows), BF16),
            sd((4, 8, PR), F32),
            sd((4, 8, PR), F32),
            sd((UNITS, 2, 2) + piece, BF16),
            sd((UNITS, 2, 2, 2, 2) + piece, BF16),
            sd((H, 3 * T, rows), BF16),
        ),
        in_specs=[hbm] * 31,
        out_specs=(hbm, hbm, vm, vm, hbm, hbm, hbm),
        scratch_shapes=[
            v((D, rows), BF16),
            v((D, rows), BF16),
            v((1, rows), jnp.int32),
            v((D,), BF16),
            v((D,), BF16),
            v((D, QKV), BF16),
            v((D, D), BF16),
            v((D, FF), BF16),
            v((D, FF), BF16),
            v((D, FF), BF16),
        ]
        + [v((PR,), F32)] * 6
        + [
            v((H, HS, rows), BF16),
            v((KV, HS, rows), BF16),
            v((KV, HS, rows), BF16),
            v((KV, rows, HS), BF16),
            v((KV, rows, HS), BF16),
            v((D, rows), BF16),
            v((D, rows), BF16),
            v((D, rows), BF16),
            v((2, 3 * T, rows), BF16),
            v((H, 1, rows), F32),
            v((D, rows), F32),
            v((D, 8), F32),
            v((4, 8, PR), F32),
            v((UNITS, 2, 2, 2, 2) + piece, BF16),
            v((UNITS, 2, 2, 2) + piece, BF16),
            v((UNITS, 2, 2) + piece, BF16),
            v((UNITS, 2) + piece, BF16),
            v((UNITS,) + piece, BF16),
            v((UNITS, bits - 1) + piece, BF16),
            v((UNITS, bits - 2) + piece, BF16),
            v((UNITS, 3, 2, 2) + piece, BF16),
            v((npeer, 4, 8, PR), F32),
            v((npeer, 4, 8, PR), F32),
            v((4, 8, PR), F32),
        ]
        + [pltpu.SemaphoreType.DMA(n if isinstance(n, tuple) else (n,)) for n in (copies, copies, 15, 15, 16, (2, 3), 2)],
        compiler_params=pltpu.CompilerParams(
            vmem_limit_bytes=VMEM_LIMIT, collective_id=0, has_side_effects=True
        ),
    )(xt, ct, seg.reshape(1, rows), g1, g2, wp, wo, wg, wu, wdt, *state, *gain_state)


VMEM_LIMIT = 63 * 2**20


def update_kernel(total, *refs):
    gf_ref, u_ref, gsum_ref, gup_ref = refs[:4]
    rows_in, state, gain_state = refs[4:6], refs[6:21], refs[21:27]
    outs = refs[27:47]
    gain_outs, rounded, gain_rounded, rows_out = refs[47:55], refs[55:60], refs[60:62], refs[62:64]
    gf, low = refs[64:66]
    held, made, wide, rows_held = refs[66:81], refs[81:101], refs[101:106], refs[106:108]
    load_sem, low_sem, gf_sem, out_sem, wide_sem, row_sem = refs[108:]

    loads = {}
    grads = []
    for t in range(4):
        grads.append(pltpu.make_async_copy(gf_ref.at[t], gf.at[t], gf_sem.at[t]))
        grads[-1].start()
    for numbers in ((0, 1, 2), (3, 4)):
        for number in numbers:
            for k in range(3):
                n = 5 * k + number
                loads[n] = pltpu.make_async_copy(state[n], held[n], load_sem.at[n])
                loads[n].start()
    lows = []
    for t in range(4):
        lows.append(pltpu.make_async_copy(u_ref.at[t], low.at[t], low_sem.at[t]))
        lows[-1].start()
    row_loads = []
    for n in range(2):
        row_loads.append(pltpu.make_async_copy(rows_in[n], rows_held[n], row_sem.at[n]))
        row_loads[-1].start()
    stores = []

    def store(src, dst, sem):
        stores.append(pltpu.make_async_copy(src, dst, sem))
        stores[-1].start()

    shard = lax.axis_index("shard")
    x = shard // 2
    for k in range(2):
        whole = jnp.concatenate([gup_ref[s, k : k + 1, :] for s in range(4)], axis=1)
        gain_rounded[k][...] = whole.astype(BF16).reshape(D)
    grad = gsum_ref[shard] / total
    for k in range(2):
        m, v, w = (gain_state[2 * q + k][...].reshape(1, PR) for q in range(3))
        one = grad[k : k + 1]
        velocity, spread, updated = adam(one, m, v, w, BASE_RATE, False)
        for q, value in enumerate((one, updated, velocity, spread)):
            gain_outs[2 * q + k][...] = value.reshape(PR)
    for t in range(4):
        numbers = ((), (), (0, 1, 2), (3, 4))[t]
        grads[t].wait()
        for number in ((0, 1, 2), (), (), (3, 4))[t]:
            for k in range(3):
                loads[5 * k + number].wait()
        for p in range(4):
            for r, lane, nl, number, r0, c0 in blocks(t, p):
                where = (slice(r0, r0 + PR), slice(c0, c0 + nl))
                m, v, w = (held[5 * k + number][where] for k in range(3))
                grad = gf[t, p // 2, p % 2, r : r + PR, lane : lane + nl].astype(F32) / total
                velocity, spread, updated = adam(grad, m, v, w, RATES[number], True)
                for q, value in enumerate((grad, updated, velocity, spread)):
                    made[5 * q + number][where] = value
        for number in numbers:
            for q in range(4):
                n = 5 * q + number
                store(made[n], outs[n], out_sem.at[n])
        lows[t].wait()
        for s in range(4):
            for p in range(4):
                for r, lane, nl, number, r0, c0 in blocks(t, p):
                    if number == 2:
                        c0 += s * (FF // 4)
                    else:
                        r0 = s * PR
                    wide[number][r0 : r0 + PR, c0 : c0 + nl] = low[
                        t, s % 2, x if s < 2 else 1 - x, p // 2, p % 2, r : r + PR, lane : lane + nl
                    ]
        for number in numbers:
            store(wide[number], rounded[number], wide_sem.at[number])
    for n in range(2):
        row_loads[n].wait()
        store(rows_held[n], rows_out[n], row_sem.at[2 + n])
    for copy in stores:
        copy.wait()


def run_update(total, bot, tgt, gf, u, gsum, gup, state, gain_state):
    vm = pl.BlockSpec(memory_space=pltpu.VMEM)
    hbm = pl.BlockSpec(memory_space=pl.ANY)
    sd = jax.ShapeDtypeStruct
    shapes = [a.shape for a in state[:5]]
    full = [(D, FF)] * 3 + [(D, QKV), (D, D)]
    return pl.pallas_call(
        lambda *refs: update_kernel(total, *refs),
        name="update",
        out_shape=tuple(sd(s, F32) for s in shapes * 4)
        + (sd((PR,), F32),) * 8
        + tuple(sd(s, BF16) for s in full)
        + (sd((D,), BF16),) * 2
        + (sd(bot.shape, BF16),) * 2,
        in_specs=[hbm, hbm, vm, vm] + [hbm] * 17 + [vm] * 6,
        out_specs=(hbm,) * 20 + (vm,) * 8 + (hbm,) * 5 + (vm,) * 2 + (hbm,) * 2,
        scratch_shapes=[
            pltpu.VMEM((UNITS, 2, 2, UNIT, LANES), BF16),
            pltpu.VMEM((UNITS, 2, 2, 2, 2, UNIT, LANES), BF16),
        ]
        + [pltpu.VMEM(s, F32) for s in shapes * 3]
        + [pltpu.VMEM(s, F32) for s in shapes * 4]
        + [pltpu.VMEM(s, BF16) for s in full]
        + [pltpu.VMEM(bot.shape, BF16)] * 2
        + [pltpu.SemaphoreType.DMA((n,)) for n in (15, 4, 4, 20, 5, 4)],
        compiler_params=pltpu.CompilerParams(vmem_limit_bytes=62 * 2**20),
    )(gf, u, gsum, gup, bot, tgt, *state, *gain_state)


def solution(mesh):
    mesh_shape = dict(mesh.shape)

    def body(
        tokens, cotangent, segment_ids, current_attention, current_project, current_output,
        current_feeding, current_gating, current_upward, current_downward, *state_all,
    ):
        rows = tokens.shape[0]
        total = float(rows * mesh_shape["rep"] * mesh_shape["shard"])
        state, gain_state = [], []
        for k in range(3):
            at, pr, ou, fe, ga, uw, dw = state_all[7 * k : 7 * k + 7]
            state += [ga, uw, dw.T, pr, ou]
            gain_state += [at, fe]
        bot, tgt, gsum, gup, gf, u, _ = run_step(
            mesh_shape, tokens.T, cotangent.T, segment_ids, current_attention, current_feeding, current_project,
            current_output, current_gating, current_upward, current_downward.T, state, gain_state,
        )
        out = run_update(total, bot, tgt, gf, u, gsum, gup, state, gain_state)
        results = [out[35].T, out[36].T]
        for q in range(4):
            ga, uw, dw, pr, ou = out[5 * q : 5 * q + 5]
            at, fe = out[20 + 2 * q : 22 + 2 * q]
            results += [at, pr, ou, fe, ga, uw, dw.T]
        ga, uw, dw, pr, ou = out[28:33]
        at, fe = out[33:35]
        return (*results, at, pr, ou, fe, ga, uw, dw.T)

    row, vec = P("shard", None), P("shard")
    seven = (vec, row, row, vec, row, row, row)
    spread = P(("shard", "rep"), None)
    in_specs = (spread, spread, P(("shard", "rep"))) + (P(),) * 7 + seven * 3
    out_specs = (spread, spread) + seven * 4 + (P(),) * 7
    return jax.shard_map(body, mesh=mesh, in_specs=in_specs, out_specs=out_specs, check_vma=False)
```

```python
import math

import jax
import jax.numpy as jnp
from jax import lax
from jax.experimental import pallas as pl
from jax.experimental.pallas import tpu as pltpu
from jax.sharding import PartitionSpec as P

D = 576
H = 9
KV = 3
HS = 64
FF = 1536
QKV = 960
STEP = 5
GROUP = H // KV

EPSILON = 1e-05
THETA = 10000.0
BETA = 0.5
ADAM_EPSILON = 1e-08
DECAY = 0.1
NEGATIVE = -1e30
BASE_RATE = 0.3

F32 = jnp.float32
BF16 = jnp.bfloat16
T = 256
PR = D // 4
LANES = 128
UNIT = 3 * PR
CH = 512
UNITS = 4


def dot(a, b):
    return jnp.dot(a, b, preferred_element_type=F32)


def dot_t(a, b):
    return lax.dot_general(a, b, (((1,), (1,)), ((), ())), preferred_element_type=F32)

MESH = pl.DeviceIdType.MESH
RATES = tuple(
    BASE_RATE * v
    for v in (float(D) ** -0.5, float(D) ** -0.5, float(FF) ** -0.5, float(D) ** -0.5, float(max(D // 96, 1)) ** -0.5)
)
CORRECTION = 1.0 - BETA**STEP


def blocks(u, p):
    if u < 3:
        c = p * (FF // 4) + u * LANES
        return [(0, 0, LANES, 0, 0, c), (PR, 0, LANES, 1, 0, c), (2 * PR, 0, LANES, 2, p * PR, u * LANES)]
    out = [(0, 0, LANES, 4, 0, p * LANES), (PR, 0, LANES, 3, 0, p * LANES)]
    if p < 3:
        return out + [(2 * PR, 0, LANES, 3, 0, 512 + p * LANES)]
    return out + [(2 * PR, 0, 64, 3, 0, 896), (2 * PR, 64, 64, 4, 0, 512)]


def adam(grad, master, moment, variance, rate, decay):
    velocity = BETA * moment + (1.0 - BETA) * grad
    spread = BETA * variance + (1.0 - BETA) * grad * grad
    direction = velocity / CORRECTION / (jnp.sqrt(spread / CORRECTION) + ADAM_EPSILON)
    if decay:
        direction = direction + DECAY * master
    return velocity, spread, master - rate * direction


def add_into(dst, a, b):
    dst[...] = (a[...].astype(F32) + b[...].astype(F32)).astype(BF16)


def column(ref, size):
    row = jnp.broadcast_to(ref[...].astype(F32).reshape(1, size), (8, size))
    return row.T[:, :1]


class Exchange:
    def __init__(self, bits, total, refs):
        self.__dict__.update(refs)
        self.bits, self.total = bits, total
        self.shard, self.rep = lax.axis_index("shard"), lax.axis_index("rep")
        self.x, self.core = self.shard // 2, lax.rem(self.shard, 2)
        self.y, self.zl = lax.rem(self.rep, 2), lax.rem(self.rep // 2, 2)
        self.peer_c = (self.flip(self.shard, 0), self.rep)
        self.peer_x = (self.flip(self.shard, 1), self.rep)
        self.peer_r = [(self.shard, self.flip(self.rep, b)) for b in range(bits)]
        self.peers = [self.peer_c, self.peer_x] + self.peer_r
        self.other = self.flip(self.shard, 1)
        self.not_x, self.not_core, self.not_y, self.not_zl = (1 - v for v in (self.x, self.core, self.y, self.zl))
        self.sent, self.kept, self.live = [], [], []

    @staticmethod
    def flip(index, bit):
        size = 1 << bit
        return index + size - 2 * size * lax.rem(index // size, 2)

    def greet(self):
        self.barrier = pltpu.get_barrier_semaphore()
        for peer in self.peers:
            pl.semaphore_signal(self.barrier, inc=1, device_id=peer, device_id_type=MESH)

    def met(self):
        pl.semaphore_wait(self.barrier, len(self.peers))

    def send(self, src, dst, peer):
        n = len(self.sent)

        def make():
            return pltpu.make_async_remote_copy(
                src_ref=src(), dst_ref=dst(), send_sem=self.send_sem.at[n], recv_sem=self.recv_sem.at[n],
                device_id=peer, device_id_type=MESH,
            )

        make().start()
        self.sent.append(make)
        return make

    def keep(self, src, dst):
        n = len(self.kept)

        def make():
            return pltpu.make_async_copy(src(), dst(), self.keep_sem.at[n])

        make().start()
        self.kept.append(make)

    def begin(self, flow, group=None):
        next(flow)
        self.live.append((flow, group))

    def tick(self, *groups):
        for entry in sorted(self.live, key=lambda e: e[1] is not None):
            if entry[1] is None or entry[1] in groups:
                try:
                    next(entry[0])
                except StopIteration:
                    self.live.remove(entry)

    def finish(self):
        turn = 1
        while self.live:
            self.tick(turn)
            turn = 1 - turn
        for copy in self.sent:
            copy().wait_send()
        for copy in self.kept:
            copy().wait()

    def load_state(self):
        for number, held in enumerate(self.held):
            for k in range(3):
                n = 5 * k + number
                yield pltpu.make_async_copy(self.state[n], held.at[k], self.st_sem.at[n])

    def have_state(self):
        for copy in self.load_state():
            copy.wait()
        for k in range(3):
            self.tail[k] = jnp.concatenate([self.held[3][k, :, 896:], self.held[4][k, :, 512:]], axis=1)

    def gain(self):
        gains, gs, gr, gu = self.gain_ref, self.gs, self.grc, self.gu
        copy = self.send(lambda: gains, lambda: gr.at[0], self.peers[0])
        yield
        last = len(self.peers) - 1
        for b in range(last + 1):
            copy().wait_recv()
            gs[b] = (gains[...] if b == 0 else gs[b - 1]) + gr[b]
            if b < last:
                copy = self.send(lambda b=b: gs.at[b], lambda b=b: gr.at[b + 1], self.peers[b + 1])
                yield
        self.gsum_ref[...] = gs[last]
        shard, other = self.shard, self.other
        grad = gs[last, shard] / self.total
        for k in range(2):
            m, v, w = (self.gain_state[2 * q + k][...].reshape(1, PR) for q in range(3))
            gu[shard, k : k + 1, :] = adam(grad[k : k + 1], m, v, w, BASE_RATE, False)[2]
        copy = self.send(lambda: gu.at[shard], lambda: gu.at[shard], self.peer_x)
        one = self.send(lambda: gu.at[shard], lambda: gu.at[shard], self.peer_c)
        yield
        copy().wait_recv()
        two = self.send(lambda: gu.at[other], lambda: gu.at[other], self.peer_c)
        yield
        one().wait_recv()
        two().wait_recv()
        self.gup_ref[...] = gu[...]

    def update(self, u, b, pieces):
        rs = slice(b * PR, (b + 1) * PR)

        def lanes(c):
            return pl.ds(c if isinstance(c, int) else pl.multiple_of(c, LANES), LANES)

        for py, pz in pieces:
            p = 2 * py + pz
            number = b if u < 3 else (4, 3, 3)[b]
            held, rate = self.held[number], RATES[number]
            if u < 3 and b == 2:
                r0 = p * PR if isinstance(p, int) else pl.multiple_of(p * PR, PR)
                state = [held[k, pl.ds(r0, PR), u * LANES : (u + 1) * LANES] for k in range(3)]
            elif u < 3:
                state = [held[k, :, lanes(p * (FF // 4) + u * LANES)] for k in range(3)]
            elif b < 2:
                state = [held[k, :, lanes(p * LANES)] for k in range(3)]
            else:
                if isinstance(p, int):
                    state = [self.tail[k] if p == 3 else held[k, :, lanes(512 + p * LANES)] for k in range(3)]
                else:
                    near = lanes(512 + jnp.minimum(p, 2) * LANES)
                    state = [jnp.where(p == 3, self.tail[k], held[k, :, near]) for k in range(3)]
                lane = lax.broadcasted_iota(jnp.int32, (PR, LANES), 1) + LANES * p
                rate = jnp.where(lane < QKV - 512, RATES[3], RATES[4])
            grad = self.agb[u, 2, py, pz, rs].astype(F32) / self.total
            self.agb[u, 0, py, pz, rs] = adam(grad, *state, rate, True)[2].astype(BF16)

    def unit(self, u, first, count):
        own = {"x": self.x, "y": self.y, "z": self.zl}
        far = {"x": self.not_x, "y": self.not_y, "z": self.not_zl}
        peer = {"x": self.peer_x, "y": self.peer_r[0], "z": self.peer_r[1]}
        core, not_core = self.core, self.not_core
        g, r1, s4, r5, agb = self.grads, self.r1, self.s4, self.r5, self.agb
        span = range(first, first + count)
        rs = pl.ds(first * PR, count * PR)

        def rows(b):
            return pl.ds(b * PR, PR)

        copy = self.send(lambda: g.at[u, :, not_core, :, :, rs], lambda: r1.at[u, :, :, :, rs], self.peer_c)
        yield
        copy().wait_recv()

        def both(n, _):
            i, p, q = n // 4, lax.rem(n // 2, 2), lax.rem(n, 2)
            add_into(g.at[u, i, core, p, q, rs], g.at[u, i, core, p, q, rs], r1.at[u, i, p, q, rs])
            return 0

        lax.fori_loop(0, 8, both, 0)

        def at(index):
            return (u, index["x"], core, index["y"], index["z"])

        for stage in range(3):
            landed = (self.r2, self.r3, self.r4)[stage]
            copies = []
            for b in span:
                order = HALVES[b]
                index = {d: own[d] for d in order[:stage]}
                index.update({d: slice(None) for d in order[stage + 1 :]})
                index[order[stage]] = far[order[stage]]
                free = (slice(None),) * (2 - stage)
                copies.append(self.send(
                    lambda w=at(index), b=b: g.at[w + (rows(b),)],
                    lambda f=free, b=b, landed=landed: landed.at[(u,) + f + (rows(b),)],
                    peer[order[stage]],
                ))
            yield
            for copy in copies:
                copy().wait_recv()
            for b in span:
                order = HALVES[b]
                later = sorted(order[stage + 1 :])
                for n in range(1 << len(later)):
                    index = {d: own[d] for d in order[: stage + 1]}
                    bits = tuple(n >> k & 1 for k in reversed(range(len(later))))
                    index.update(zip(later, bits))
                    w = at(index) + (rows(b),)
                    if stage < 2:
                        add_into(g.at[w], g.at[w], landed.at[(u,) + bits + (rows(b),)])
                    else:
                        add_into(s4.at[u, 0, rows(b)], g.at[w], landed.at[u, rows(b)])

        last = self.bits - 2
        for k in range(last):
            copy = self.send(lambda k=k: s4.at[u, k, rs], lambda k=k: r5.at[u, k, rs], self.peer_r[2 + k])
            yield
            copy().wait_recv()
            add_into(s4.at[u, k + 1, rs], s4.at[u, k, rs], r5.at[u, k, rs])
        y, zl = self.y, self.zl
        agb[u, 2, y, zl, rs] = s4[u, last, rs]

        for stage in range(3):
            copies = []
            for b in span:
                order = GATHERS[b]
                d = order[stage]
                known = order[:stage]
                index = (slice(None) if "y" in known else y, slice(None) if "z" in known else zl, rows(b))
                if d == "x":
                    ys = range(2) if "y" in known else (y,)
                    zs = range(2) if "z" in known else (zl,)
                    self.update(u, b, [(i, j) for i in ys for j in zs])
                    copies.append(self.send(
                        lambda w=index: agb.at[(u, 0) + w], lambda w=index: agb.at[(u, 1) + w], peer[d]
                    ))
                    continue
                kinds = pl.ds(1, 2) if "x" in known else 2
                copies.append(self.send(
                    lambda w=index, k=kinds: agb.at[(u, k) + w], lambda w=index, k=kinds: agb.at[(u, k) + w], peer[d]
                ))
            yield
            for copy in copies:
                copy().wait_recv()
        self.keep(lambda: agb.at[u, 2, :, :, rs], lambda: self.gf_ref.at[u, :, :, rs])
        for b in span:
            known = GATHERS[b][: GATHERS[b].index("x")]
            if known == "":
                self.update(u, b, [(self.not_y, zl), (y, self.not_zl), (self.not_y, self.not_zl)])
            elif known == "y":
                self.update(u, b, [(i, self.not_zl) for i in range(2)])
            elif known == "z":
                self.update(u, b, [(self.not_y, i) for i in range(2)])
        self.keep(lambda: agb.at[u, pl.ds(0, 2), :, :, rs], lambda: self.u_ref.at[u, core, :, :, :, rs])
        copy = self.send(
            lambda: agb.at[u, pl.ds(0, 2), :, :, rs], lambda: self.u_ref.at[u, core, :, :, :, rs], self.peer_c
        )
        yield
        copy().wait_recv()


HALVES = ("xyz", "yzx", "zxy")
GATHERS = ("zyx", "xzy", "yxz")


def step_kernel(bits, total, *refs):
    ins, state = refs[:10], refs[10:25]
    bot_ref, tgt_ref, gsum_ref, gup_ref, gf_ref, u_ref, e_hbm = refs[31:38]
    (
        xt_ref, ct_ref, seg_ref, g1_ref, g2_ref, wp_ref, wo_ref, wg_ref, wu_ref, wdt_ref, *gain_state,
        qt, kt_, vt, kn, vn, nt, mt, gmt, es, invl, gres, dgain, gain_ref,
        grads, r1, r2, r3, r4, s4, r5, agb, gs, grc, gu,
        send_sem, recv_sem, keep_sem, st_sem, in_sem, e_sem, out_sem,
    ) = refs[38:]
    rows = xt_ref.shape[1]
    tiles = rows // T
    half = HS // 2
    ex = Exchange(bits, total, dict(
        state=state, gain_state=gain_state, gsum_ref=gsum_ref, gup_ref=gup_ref, gf_ref=gf_ref, u_ref=u_ref,
        gain_ref=gain_ref, grads=grads, r1=r1, r2=r2, r3=r3, r4=r4, s4=s4, r5=r5, agb=agb, gs=gs, grc=grc, gu=gu,
        send_sem=send_sem, recv_sem=recv_sem, keep_sem=keep_sem, st_sem=st_sem,
    ))

    loads = [
        pltpu.make_async_copy(src, dst, in_sem.at[n])
        for n, (src, dst) in enumerate(zip(
            tuple(ins) + tuple(refs[25:31]),
            (xt_ref, ct_ref, seg_ref, g1_ref, g2_ref, wp_ref, wo_ref, wg_ref, wu_ref, wdt_ref, *gain_state),
        ))
    ]
    for n in (2, 3, 0, 5, 6, 1, 4, 7, 8, 9, 10, 11, 12, 13, 14, 15):
        loads[n].start()
    ex.greet()
    loads[2].wait()

    seg_row = seg_ref[...].astype(F32)
    seg_cols = jnp.broadcast_to(seg_row, (8, rows)).T[:, :1]
    starts = jnp.zeros((1, rows), F32)
    for k in range(0, rows, 128):
        lower = (seg_cols[k : k + 128] < seg_row).astype(F32)
        starts = starts + jnp.sum(lower, axis=0, keepdims=True)
    places_row = lax.broadcasted_iota(jnp.int32, (1, rows), 1).astype(F32)
    index = lax.broadcasted_iota(jnp.int32, (half, 1), 0).astype(F32)
    frequency = jnp.exp(index * (-2.0 * math.log(THETA) / HS))
    angles = frequency * (places_row - starts)
    cosine = jnp.cos(angles)
    sine = jnp.sin(angles)

    loads[3].wait()
    gain1 = column(g1_ref, D)
    loads[5].wait()
    loads[0].wait()
    dgain[...] = jnp.zeros_like(dgain)

    def unit_one(cols):
        xf = xt_ref[:, cols].astype(F32)
        scale = lax.rsqrt(jnp.mean(xf * xf, axis=0, keepdims=True) + EPSILON)
        return xf * scale, scale

    def project(wpt):
        wpt[...] = wp_ref[...].T
        for r in range(tiles):
            r0 = r * T
            cs = cosine[:, r0 : r0 + T]
            sn = sine[:, r0 : r0 + T]
            unit, _ = unit_one(slice(r0, r0 + T))
            normed = (unit * gain1).astype(BF16)
            nt[:, r0 : r0 + T] = normed
            joined = dot(wpt[...], normed)
            for h in range(H + 2 * KV):
                jt = joined[h * HS : (h + 1) * HS]
                a = jt[:half]
                b = jt[half:]
                if h < H:
                    qt[h, 0:half, r0 : r0 + T] = ((a * cs - b * sn) * (HS**-0.5)).astype(BF16)
                    qt[h, half:HS, r0 : r0 + T] = ((b * cs + a * sn) * (HS**-0.5)).astype(BF16)
                elif h < H + KV:
                    kt_[h - H, 0:half, r0 : r0 + T] = (a * cs - b * sn).astype(BF16)
                    kt_[h - H, half:HS, r0 : r0 + T] = (b * cs + a * sn).astype(BF16)
                else:
                    vt[h - H - KV, :, r0 : r0 + T] = jt.astype(BF16)

    pl.run_scoped(project, pltpu.VMEM((QKV, D), BF16))
    for n in range(KV):
        kn[n] = kt_[n].T
        vn[n] = vt[n].T

    def ef(k, i):
        if k < 2:
            return k * T, i * T
        return 2 * T, (i - 2 + 2 * (k - 2)) * T

    def e_copies(h, out):
        slot = h % 2 if isinstance(h, int) else lax.rem(h, 2)
        for n in range(3):
            here, there = es.at[slot, pl.ds(n * T, T)], e_hbm.at[h, pl.ds(n * T, T)]
            pair = (here, there) if out else (there, here)
            yield pltpu.make_async_copy(*pair, e_sem.at[slot, n])

    def e_start(h, out):
        for copy in e_copies(h, out):
            copy.start()

    def e_wait(h, out):
        for copy in e_copies(h, out):
            copy.wait()

    def forward(bias, sc):
        for i in range(tiles):
            for k in range(i + 1):
                kk = lax.broadcasted_iota(jnp.int32, (T, T), 0).astype(F32) + float(k * T)
                ok = kk >= starts[:, i * T : (i + 1) * T]
                if k == i:
                    qq = lax.broadcasted_iota(jnp.int32, (T, T), 1).astype(F32) + float(i * T)
                    ok = ok & (kk <= qq)
                bias[i * (i + 1) // 2 + k] = jnp.where(ok, 0.0, NEGATIVE)

        def head(h, _):
            n = h // GROUP
            slot = lax.rem(h, 2)

            @pl.when(h >= 2)
            def _():
                e_wait(h - 2, True)

            for i in range(tiles):
                q = qt[h, :, i * T : (i + 1) * T]
                peak = None
                for k in range(i + 1):
                    s = dot(kn[n, k * T : (k + 1) * T, :], q) + bias[i * (i + 1) // 2 + k]
                    sc[i % 2, k] = s
                    top = jnp.max(s, axis=0, keepdims=True)
                    peak = top if peak is None else jnp.maximum(peak, top)
                total_ = jnp.zeros((1, T), F32)
                out = jnp.zeros((HS, T), F32)
                for k in range(i + 1):
                    e = jnp.exp(sc[i % 2, k] - peak)
                    total_ = total_ + jnp.sum(e, axis=0, keepdims=True)
                    e16 = e.astype(BF16)
                    a, b = ef(k, i)
                    es[slot, a : a + T, b : b + T] = e16
                    out = out + dot(vt[n, :, k * T : (k + 1) * T], e16)
                inverse = 1.0 / total_
                invl[h, :, i * T : (i + 1) * T] = inverse
                mt[pl.ds(pl.multiple_of(h * HS, HS), HS), i * T : (i + 1) * T] = (
                    out * inverse
                ).astype(BF16)
            e_start(h, True)
            return 0

        lax.fori_loop(0, H, head, 0)
        e_wait(H - 2, True)
        e_wait(H - 1, True)

    pl.run_scoped(
        forward,
        pltpu.VMEM((tiles * (tiles + 1) // 2, T, T), F32),
        pltpu.VMEM((2, tiles, T, T), F32),
    )
    e_start(0, False)
    ex.met()

    RT = 512
    CT = 256

    def feeding(wot, cn, n2, n2t, hid, gg, gu_, res, scale2):
        for n in (1, 4, 6, 7, 8, 9, 10, 11, 12, 13, 14, 15):
            loads[n].wait()
        gain2 = column(g2_ref, D)
        wot[...] = wo_ref[...].T
        cn[...] = ct_ref[...].T

        def mixing(r, _):
            rs = pl.ds(pl.multiple_of(r * T, T), T)
            residual = xt_ref[:, rs].astype(F32) + dot(wot[...], mt[:, rs])
            scale = lax.rsqrt(jnp.mean(residual * residual, axis=0, keepdims=True) + EPSILON)
            res[:, rs] = residual
            scale2[:, rs] = scale
            n2v = (residual * scale * gain2).astype(BF16)
            n2t[:, rs] = n2v
            n2[rs, :] = n2v.T
            return 0

        lax.fori_loop(0, rows // T, mixing, 0)
        def part_of(ref, u, s0, s1):
            return jnp.concatenate(
                [ref[:, s * (FF // 4) + u * LANES : s * (FF // 4) + (u + 1) * LANES] for s in range(s0, s1)], axis=1
            )

        for u in range(3):

            for half_ in range(2):
                js = slice(half_ * CT, (half_ + 1) * CT)

                def tile(r, _):
                    rs = pl.ds(pl.multiple_of(r * RT, RT), RT)
                    gate = dot(n2[rs, :], part_of(wg_ref, u, 2 * half_, 2 * half_ + 2))
                    up_ = dot(n2[rs, :], part_of(wu_ref, u, 2 * half_, 2 * half_ + 2))
                    gh = dot(cn[rs, :], part_of(wdt_ref, u, 2 * half_, 2 * half_ + 2))
                    sg = 0.5 * jnp.tanh(0.5 * gate) + 0.5
                    sl = gate * sg
                    hid[rs, js] = (sl * up_).astype(BF16)
                    gg[rs, js] = (gh * up_ * (sg + sl * (1.0 - sg))).astype(BF16)
                    gu_[rs, js] = (gh * sl).astype(BF16)
                    return 0

                lax.fori_loop(0, rows // RT, tile, 0)
                if u and half_:
                    ex.tick(0, 1)
            for b, (left, right) in enumerate(((n2t, gg), (n2t, gu_), (ct_ref, hid))):
                part = dot(left[...], right[...]).astype(BF16)
                for s in range(4):
                    for p in range(4):
                        a, c = (s, p) if b < 2 else (p, s)
                        grads[u, s // 2, s % 2, p // 2, p % 2, b * PR : (b + 1) * PR, :] = part[
                            a * PR : (a + 1) * PR, c * LANES : (c + 1) * LANES
                        ]
            ex.begin(ex.unit(u, 0, 3), u % 2)

            def back(r, _):
                rs = pl.ds(pl.multiple_of(r * RT, RT), RT)
                gn2 = dot_t(part_of(wg_ref, u, 0, 4), gg[rs, :]) + dot_t(part_of(wu_ref, u, 0, 4), gu_[rs, :])
                gres[:, rs] = gn2 if u == 0 else gres[:, rs] + gn2
                res[:, rs] += dot_t(part_of(wdt_ref, u, 0, 4), hid[rs, :])
                return 0

            lax.fori_loop(0, rows // RT, back, 0)
            if u < 2:
                ex.tick(0, 1)

        def ending(r, _):
            rs = pl.ds(pl.multiple_of(r * T, T), T)
            n2t[:, rs] = res[:, rs].astype(BF16)
            scale = scale2[:, rs]
            residual = xt_ref[:, rs].astype(F32) + dot(wot[...], mt[:, rs])
            unit = residual * scale
            gn2 = gres[:, rs]
            dgain[:, 1:2] += jnp.sum(gn2 * unit, axis=1, keepdims=True)
            e = gn2 * gain2
            gr = ct_ref[:, rs].astype(F32) + scale * (
                e - unit * jnp.mean(e * unit, axis=0, keepdims=True)
            )
            gres[:, rs] = gr
            gmt[:, rs] = dot(wo_ref[...], gr.astype(BF16)).astype(BF16)
            return 0

        lax.fori_loop(0, rows // T, ending, 0)
        out = pltpu.make_async_copy(n2t, bot_ref, out_sem.at[0])
        out.start()
        part = dot_t(mt[...], gres[...].astype(BF16)).astype(BF16)
        for s in range(4):
            mine = part[s * PR : (s + 1) * PR]
            for p in range(4):
                grads[3, s // 2, s % 2, p // 2, p % 2, :PR, :] = mine[:, p * LANES : (p + 1) * LANES]
            grads[3, s // 2, s % 2, 1, 1, 2 * PR :, 64:] = mine[:, 512:]
        out.wait()

    pl.run_scoped(
        feeding,
        pltpu.VMEM((D, D), BF16),
        pltpu.VMEM((rows, D), BF16),
        pltpu.VMEM((rows, D), BF16),
        pltpu.VMEM((D, rows), BF16),
        pltpu.VMEM((rows, CH), BF16),
        pltpu.VMEM((rows, CH), BF16),
        pltpu.VMEM((rows, CH), BF16),
        pltpu.VMEM((D, rows), F32),
        pltpu.VMEM((1, rows), F32),
    )
    def backward(ds, gjt, dk, dv, cs_ref, sn_ref, tail, *held):
        ex.held, ex.tail = held, tail
        for copy in ex.load_state():
            copy.start()
        cs_ref[...] = cosine
        sn_ref[...] = sine

        def unrotate(v, base):
            a = v[:half]
            b = v[half:]
            cs = cs_ref[...]
            sn = sn_ref[...]
            gjt[base : base + half, :] = (a * cs + b * sn).astype(BF16)
            gjt[base + half : base + HS, :] = (b * cs - a * sn).astype(BF16)

        def head(h, n):
            slot = h % 2
            hs = slice(h * HS, (h + 1) * HS)
            if h + 1 < H:
                e_start(h + 1, False)

            do = (gmt[hs, :].astype(F32) * invl[h]).astype(BF16)
            delta = jnp.sum(do.astype(F32) * mt[hs, :].astype(F32), axis=0, keepdims=True)
            e_wait(h, False)
            for k in range(tiles):
                ks = slice(k * T, (k + 1) * T)
                for i in range(k, tiles):
                    cols = slice(i * T, (i + 1) * T)
                    a, b = ef(k, i)
                    dp = dot(vn[n, ks, :], do[:, cols]) - delta[:, cols]
                    ds[ks, cols] = (es[slot, a : a + T, b : b + T].astype(F32) * dp).astype(BF16)
                a, b = ef(k, k)
                dv[ks, :] += dot_t(es[slot, a : a + T, b : b + rows - k * T], do[:, k * T :])
                dk[ks, :] += dot_t(ds[ks, k * T :], qt[h, :, k * T :])
            dq = [
                dot(kt_[n, :, : (i + 1) * T], ds[: (i + 1) * T, i * T : (i + 1) * T])
                for i in range(tiles)
            ]
            unrotate(jnp.concatenate(dq, axis=1) * (HS**-0.5), h * HS)

        for n in range(KV):
            dk[...] = jnp.zeros_like(dk)
            dv[...] = jnp.zeros_like(dv)
            for g in range(GROUP):
                head(n * GROUP + g, n)
                if n * GROUP + g == 0:
                    ex.have_state()
                if n * GROUP + g in (0, 3, 6, 8):
                    ex.tick(0, 1)
            unrotate(dk[...].T, H * HS + n * HS)
            gjt[(H + KV + n) * HS : (H + KV + n + 1) * HS, :] = dv[...].T.astype(BF16)

        for k in range(2):
            part = dot_t(nt[...], gjt[512 * k : min(512 * k + 512, QKV), :]).astype(BF16)
            for s in range(4):
                mine = part[s * PR : (s + 1) * PR]
                for p in range(4):
                    c = p * LANES
                    w = min(part.shape[1] - c, LANES)
                    grads[3, s // 2, s % 2, p // 2, p % 2, (k + 1) * PR : (k + 2) * PR, :w] = mine[
                        :, c : c + w
                    ]
        ex.begin(ex.unit(3, 0, 3))

        for r in range(tiles):
            rs = slice(r * T, (r + 1) * T)
            gn = dot(wp_ref[...], gjt[:, rs])
            unit, scale = unit_one(rs)
            dgain[:, 0:1] += jnp.sum(gn * unit, axis=1, keepdims=True)
            e = gn * gain1
            tg = gres[:, rs] + scale * (e - unit * jnp.mean(e * unit, axis=0, keepdims=True))
            gmt[:, rs] = tg.astype(BF16)
            if r == 1:
                ex.tick(0, 1)
        out = pltpu.make_async_copy(gmt, tgt_ref, out_sem.at[1])
        out.start()
        for s in range(4):
            gain_ref[s] = dgain[s * PR : (s + 1) * PR, :].T
        ex.begin(ex.gain())
        ex.finish()
        out.wait()

    pl.run_scoped(
        backward,
        pltpu.VMEM((rows, rows), BF16),
        pltpu.VMEM((QKV, rows), BF16),
        pltpu.VMEM((rows, HS), F32),
        pltpu.VMEM((rows, HS), F32),
        pltpu.VMEM((half, rows), F32),
        pltpu.VMEM((half, rows), F32),
        pltpu.VMEM((3, PR, LANES), F32),
        *[pltpu.VMEM((3,) + a.shape, F32) for a in state[:5]],
    )


def run_step(mesh_shape, xt, ct, seg, g1, g2, wp, wo, wg, wu, wdt, state, gain_state):
    rows = xt.shape[1]
    bits = mesh_shape["rep"].bit_length() - 1
    total = float(rows * mesh_shape["rep"] * mesh_shape["shard"])
    vm = pl.BlockSpec(memory_space=pltpu.VMEM)
    hbm = pl.BlockSpec(memory_space=pl.ANY)
    sd = jax.ShapeDtypeStruct
    npeer = bits + 2
    copies = 5 * 24 + 5 * bits + npeer + 3
    piece = (UNIT, LANES)
    v = pltpu.VMEM
    return pl.pallas_call(
        lambda *refs: step_kernel(bits, total, *refs),
        name="step",
        out_shape=(
            sd((D, rows), BF16),
            sd((D, rows), BF16),
            sd((4, 8, PR), F32),
            sd((4, 8, PR), F32),
            sd((UNITS, 2, 2) + piece, BF16),
            sd((UNITS, 2, 2, 2, 2) + piece, BF16),
            sd((H, 3 * T, rows), BF16),
        ),
        in_specs=[hbm] * 31,
        out_specs=(hbm, hbm, vm, vm, hbm, hbm, hbm),
        scratch_shapes=[
            v((D, rows), BF16),
            v((D, rows), BF16),
            v((1, rows), jnp.int32),
            v((D,), BF16),
            v((D,), BF16),
            v((D, QKV), BF16),
            v((D, D), BF16),
            v((D, FF), BF16),
            v((D, FF), BF16),
            v((D, FF), BF16),
        ]
        + [v((PR,), F32)] * 6
        + [
            v((H, HS, rows), BF16),
            v((KV, HS, rows), BF16),
            v((KV, HS, rows), BF16),
            v((KV, rows, HS), BF16),
            v((KV, rows, HS), BF16),
            v((D, rows), BF16),
            v((D, rows), BF16),
            v((D, rows), BF16),
            v((2, 3 * T, rows), BF16),
            v((H, 1, rows), F32),
            v((D, rows), F32),
            v((D, 8), F32),
            v((4, 8, PR), F32),
            v((UNITS, 2, 2, 2, 2) + piece, BF16),
            v((UNITS, 2, 2, 2) + piece, BF16),
            v((UNITS, 2, 2) + piece, BF16),
            v((UNITS, 2) + piece, BF16),
            v((UNITS,) + piece, BF16),
            v((UNITS, bits - 1) + piece, BF16),
            v((UNITS, bits - 2) + piece, BF16),
            v((UNITS, 3, 2, 2) + piece, BF16),
            v((npeer, 4, 8, PR), F32),
            v((npeer, 4, 8, PR), F32),
            v((4, 8, PR), F32),
        ]
        + [pltpu.SemaphoreType.DMA(n if isinstance(n, tuple) else (n,)) for n in (copies, copies, 15, 15, 16, (2, 3), 2)],
        compiler_params=pltpu.CompilerParams(
            vmem_limit_bytes=VMEM_LIMIT, collective_id=0, has_side_effects=True
        ),
    )(xt, ct, seg.reshape(1, rows), g1, g2, wp, wo, wg, wu, wdt, *state, *gain_state)


VMEM_LIMIT = 63 * 2**20


def update_kernel(total, *refs):
    gf_ref, u_ref, gsum_ref, gup_ref = refs[:4]
    rows_in, state, gain_state = refs[4:6], refs[6:21], refs[21:27]
    outs = refs[27:47]
    gain_outs, rounded, gain_rounded, rows_out = refs[47:55], refs[55:60], refs[60:62], refs[62:64]
    gf, low = refs[64:66]
    held, made, wide, rows_held = refs[66:81], refs[81:101], refs[101:106], refs[106:108]
    load_sem, low_sem, gf_sem, out_sem, wide_sem, row_sem = refs[108:]

    loads = {}
    grads = []
    for t in range(4):
        grads.append(pltpu.make_async_copy(gf_ref.at[t], gf.at[t], gf_sem.at[t]))
        grads[-1].start()
    for numbers in ((0, 1, 2), (3, 4)):
        for number in numbers:
            for k in range(3):
                n = 5 * k + number
                loads[n] = pltpu.make_async_copy(state[n], held[n], load_sem.at[n])
                loads[n].start()
    lows = []
    for t in range(4):
        lows.append(pltpu.make_async_copy(u_ref.at[t], low.at[t], low_sem.at[t]))
        lows[-1].start()
    row_loads = []
    for n in range(2):
        row_loads.append(pltpu.make_async_copy(rows_in[n], rows_held[n], row_sem.at[n]))
        row_loads[-1].start()
    stores = []

    def store(src, dst, sem):
        stores.append(pltpu.make_async_copy(src, dst, sem))
        stores[-1].start()

    shard = lax.axis_index("shard")
    x = shard // 2
    for k in range(2):
        whole = jnp.concatenate([gup_ref[s, k : k + 1, :] for s in range(4)], axis=1)
        gain_rounded[k][...] = whole.astype(BF16).reshape(D)
    grad = gsum_ref[shard] / total
    for k in range(2):
        m, v, w = (gain_state[2 * q + k][...].reshape(1, PR) for q in range(3))
        one = grad[k : k + 1]
        velocity, spread, updated = adam(one, m, v, w, BASE_RATE, False)
        for q, value in enumerate((one, updated, velocity, spread)):
            gain_outs[2 * q + k][...] = value.reshape(PR)
    for t in range(4):
        numbers = ((), (), (0, 1, 2), (3, 4))[t]
        grads[t].wait()
        for number in ((0, 1, 2), (), (), (3, 4))[t]:
            for k in range(3):
                loads[5 * k + number].wait()
        for p in range(4):
            for r, lane, nl, number, r0, c0 in blocks(t, p):
                where = (slice(r0, r0 + PR), slice(c0, c0 + nl))
                m, v, w = (held[5 * k + number][where] for k in range(3))
                grad = gf[t, p // 2, p % 2, r : r + PR, lane : lane + nl].astype(F32) / total
                velocity, spread, updated = adam(grad, m, v, w, RATES[number], True)
                for q, value in enumerate((grad, updated, velocity, spread)):
                    made[5 * q + number][where] = value
        for number in numbers:
            for q in range(4):
                n = 5 * q + number
                store(made[n], outs[n], out_sem.at[n])
        lows[t].wait()
        for s in range(4):
            for p in range(4):
                for r, lane, nl, number, r0, c0 in blocks(t, p):
                    if number == 2:
                        c0 += s * (FF // 4)
                    else:
                        r0 = s * PR
                    wide[number][r0 : r0 + PR, c0 : c0 + nl] = low[
                        t, s % 2, x if s < 2 else 1 - x, p // 2, p % 2, r : r + PR, lane : lane + nl
                    ]
        for number in numbers:
            store(wide[number], rounded[number], wide_sem.at[number])
    for n in range(2):
        row_loads[n].wait()
        store(rows_held[n], rows_out[n], row_sem.at[2 + n])
    for copy in stores:
        copy.wait()


def run_update(total, bot, tgt, gf, u, gsum, gup, state, gain_state):
    vm = pl.BlockSpec(memory_space=pltpu.VMEM)
    hbm = pl.BlockSpec(memory_space=pl.ANY)
    sd = jax.ShapeDtypeStruct
    shapes = [a.shape for a in state[:5]]
    full = [(D, FF)] * 3 + [(D, QKV), (D, D)]
    return pl.pallas_call(
        lambda *refs: update_kernel(total, *refs),
        name="update",
        out_shape=tuple(sd(s, F32) for s in shapes * 4)
        + (sd((PR,), F32),) * 8
        + tuple(sd(s, BF16) for s in full)
        + (sd((D,), BF16),) * 2
        + (sd(bot.shape, BF16),) * 2,
        in_specs=[hbm, hbm, vm, vm] + [hbm] * 17 + [vm] * 6,
        out_specs=(hbm,) * 20 + (vm,) * 8 + (hbm,) * 5 + (vm,) * 2 + (hbm,) * 2,
        scratch_shapes=[
            pltpu.VMEM((UNITS, 2, 2, UNIT, LANES), BF16),
            pltpu.VMEM((UNITS, 2, 2, 2, 2, UNIT, LANES), BF16),
        ]
        + [pltpu.VMEM(s, F32) for s in shapes * 3]
        + [pltpu.VMEM(s, F32) for s in shapes * 4]
        + [pltpu.VMEM(s, BF16) for s in full]
        + [pltpu.VMEM(bot.shape, BF16)] * 2
        + [pltpu.SemaphoreType.DMA((n,)) for n in (15, 4, 4, 20, 5, 4)],
        compiler_params=pltpu.CompilerParams(vmem_limit_bytes=62 * 2**20),
    )(gf, u, gsum, gup, bot, tgt, *state, *gain_state)


def solution(mesh):
    mesh_shape = dict(mesh.shape)

    def body(
        tokens, cotangent, segment_ids, current_attention, current_project, current_output,
        current_feeding, current_gating, current_upward, current_downward, *state_all,
    ):
        rows = tokens.shape[0]
        total = float(rows * mesh_shape["rep"] * mesh_shape["shard"])
        state, gain_state = [], []
        for k in range(3):
            at, pr, ou, fe, ga, uw, dw = state_all[7 * k : 7 * k + 7]
            state += [ga, uw, dw.T, pr, ou]
            gain_state += [at, fe]
        bot, tgt, gsum, gup, gf, u, _ = run_step(
            mesh_shape, tokens.T, cotangent.T, segment_ids, current_attention, current_feeding, current_project,
            current_output, current_gating, current_upward, current_downward.T, state, gain_state,
        )
        out = run_update(total, bot, tgt, gf, u, gsum, gup, state, gain_state)
        results = [out[35].T, out[36].T]
        for q in range(4):
            ga, uw, dw, pr, ou = out[5 * q : 5 * q + 5]
            at, fe = out[20 + 2 * q : 22 + 2 * q]
            results += [at, pr, ou, fe, ga, uw, dw.T]
        ga, uw, dw, pr, ou = out[28:33]
        at, fe = out[33:35]
        return (*results, at, pr, ou, fe, ga, uw, dw.T)

    row, vec = P("shard", None), P("shard")
    seven = (vec, row, row, vec, row, row, row)
    spread = P(("shard", "rep"), None)
    in_specs = (spread, spread, P(("shard", "rep"))) + (P(),) * 7 + seven * 3
    out_specs = (spread, spread) + seven * 4 + (P(),) * 7
    return jax.shard_map(body, mesh=mesh, in_specs=in_specs, out_specs=out_specs, check_vma=False)
```
